256 devices in a mesh: refresh: 8 (over z), lists: 32 (over y, x, core).
Axes of the slice: x: 4, y: 4, z: 8, core: 2. Of those that a mesh axis runs over, the one named last changes fastest.
Arguments:
- features: bfloat16 [131072, 1024], P(('refresh', 'lists')), may hold values from -6 to 6
- w_hidden: bfloat16 [1024, 1024], P('refresh'), may hold values from -0.1875 to 0.1875
- w_out: bfloat16 [1024, 256], P('refresh'), may hold values from -0.1875 to 0.1875
- list_ids: int32 [131072], P(('refresh', 'lists')), may hold values from 0 to 4095, as said below
- centroids: bfloat16 [4096, 256], P('lists'), may hold values from -6 to 6
- queries: bfloat16 [16384, 256], P('lists'), may hold values from -0.5 to 0.5
Outputs:
- stored_codes: bfloat16 [262144, 256], P(('refresh', 'lists'))
- best: float32 [256, 16384], P(('refresh', 'lists'))
The draws below stay inside these ranges and needn't reach their ends.
Inputs may be any that keep to these rules, and one draw needn't show every extreme that they name: `list_ids`: among the 512 items of one device, the items whose list lies in owner j's range (128 * j to 128 * j + 127) number at most 32 for every owner j, and exactly 32 for one owner.
All inputs are finite; a program needn't handle non-finite values.
Results may differ from the reference program's by a relative error of at most 0.007.
Values may be sent and summed in bfloat16 or wider, within the bound.
A program may use at most 64 MiB of HBM per device.

```python
import jax
import jax.numpy as jnp
from jax import lax

FEAT = 1024
D_OUT = 256
LISTS_DEV = 128
ITEM_DEV = 512
OWNERS = 32
CAP = 32
ITEMS = 131072
LISTS = 4096
QUERIES = 16384
DEVICES = 256


def draw_list_ids(key, part):
    key = jax.random.fold_in(key, 7)
    slots_all = OWNERS * CAP
    counter = jnp.arange(slots_all, dtype=jnp.int32)
    slot_owner = counter // CAP

    def one_block(index):
        block_key = jax.random.fold_in(key, index)
        hot_key, order_key, shuffle_key, local_key = jax.random.split(block_key, 4)
        hottest = jax.random.randint(hot_key, (), 0, OWNERS)
        shuffled = jax.random.randint(order_key, (slots_all,), 0, 2 ** 15) * slots_all + counter + slots_all
        ordering = jnp.where(slot_owner == hottest, counter, shuffled)
        picked = slot_owner[jnp.argsort(ordering)[:ITEM_DEV]]
        owners_drawn = picked[jax.random.permutation(shuffle_key, ITEM_DEV)]
        within = jax.random.randint(local_key, (ITEM_DEV,), 0, LISTS_DEV)
        return owners_drawn * LISTS_DEV + within
    return jax.vmap(one_block)(jnp.arange(ITEMS // ITEM_DEV)).reshape(-1).astype(jnp.int32)


def steps_of(stream_key, extent, shards, low, high):
    def one(position, shards_of):
        steps = jax.random.uniform(jax.random.fold_in(jax.random.fold_in(stream_key, 6), position), (shards_of,), jnp.float32, low / len(shards), high / len(shards))
        return jnp.repeat(jnp.exp(steps), extent[position] // shards_of).reshape((-1,) + (1,) * (len(extent) - position - 1))

    level = one(*shards[0])
    for cut in shards[1:]:
        level = level * one(*cut)
    return level


def centred(rng, extent, deviation, most, cuts=(), kind=jnp.bfloat16):
    result = jax.random.normal(rng, extent, jnp.float32) * deviation
    if len(cuts) > 0:
        result = steps_of(rng, extent, cuts, -0.22, 0.18) * result
    return jnp.clip(result, min=-most, max=most).astype(kind)


def setup_inputs(seed: int = 0) -> dict:
    splits = jax.random.split(jax.random.key(seed), 7)
    return {
        "features": centred(splits[0], (ITEMS, FEAT), 1.0, 6.0, ((0, 256),)),
        "w_hidden": centred(splits[1], (FEAT, FEAT), FEAT ** -0.5, 0.1875, ((0, 8),)),
        "w_out": centred(splits[2], (FEAT, D_OUT), FEAT ** -0.5, 0.1875, ((0, 8),)),
        "list_ids": draw_list_ids(jax.random.fold_in(splits[6], 71), 0),
        "centroids": centred(splits[4], (LISTS, D_OUT), 1.0, 6.0, ((0, 32),)),
        "queries": centred(splits[5], (QUERIES, D_OUT), 0.0625, 0.5, ((0, 32),)),
    }


def root_scale(values):
    return values * lax.rsqrt(lax.optimization_barrier(jnp.mean(values * values, axis=-1, keepdims=True)) + 1e-06)

def best_for(query_block, block_codes, block_lists):
    direct = jnp.dot(query_block, block_codes.T, preferred_element_type=jnp.float32)
    filled = block_lists >= 0
    return lax.optimization_barrier(jnp.max(jnp.where(filled[None, :], direct, -1e+30), axis=1))

def reference(features, w_hidden, w_out, list_ids, centroids, queries):
    inputs = features.astype(jnp.float32)
    normed = root_scale(inputs).astype(jnp.bfloat16)
    pre = jnp.dot(normed, w_hidden, preferred_element_type=jnp.float32)
    hidden = (inputs + jax.nn.gelu(pre, approximate=False)).astype(jnp.bfloat16)
    hnorm = root_scale(hidden.astype(jnp.float32)).astype(jnp.bfloat16)
    vectors = jnp.dot(hnorm, w_out, preferred_element_type=jnp.float32).astype(jnp.bfloat16)
    positions = jnp.arange(ITEMS, dtype=jnp.int32)
    device = positions // ITEM_DEV
    group = device // OWNERS
    source = device % OWNERS
    owner = list_ids // LISTS_DEV
    owner_table = (owner[:, None] == jnp.arange(OWNERS, dtype=jnp.int32)[None, :]).astype(jnp.int32)
    blocks = owner_table.reshape(DEVICES, ITEM_DEV, OWNERS)
    prior = jnp.cumsum(blocks, axis=1) - blocks
    ranking = lax.optimization_barrier(jnp.sum(prior * blocks, axis=2)).reshape(ITEMS).astype(jnp.int32)
    slots_dev = OWNERS * CAP
    target = (group * OWNERS + owner) * slots_dev + source * CAP + ranking
    residual = vectors.astype(jnp.float32) - centroids[list_ids].astype(jnp.float32)
    buffer_rows = jnp.zeros((DEVICES * slots_dev, D_OUT), jnp.float32).at[target].set(residual)
    local = list_ids - owner * LISTS_DEV
    buffer_lists = jnp.full((DEVICES * slots_dev,), -1, jnp.int32).at[target].set(local)
    stored_codes = buffer_rows.astype(jnp.bfloat16)

    def score_one(group_args):
        return best_for(queries, group_args[0], group_args[1])
    best = lax.map(score_one, (stored_codes.reshape(DEVICES, slots_dev, D_OUT), buffer_lists.reshape(DEVICES, slots_dev)))
    return (stored_codes, best)
```

```python
import jax
import jax.numpy as jnp
from jax import lax
from jax.experimental import pallas as pl
from jax.experimental.pallas import tpu as pltpu
from jax.sharding import PartitionSpec as P

MESH = pl.DeviceIdType.MESH
NY, NX, NC, NZ = 4, 4, 2, 8
PLANE = NY * NX * NC
ITEMS, FEAT, WIDTH, LISTS, CAP = 512, 1024, 256, 128, 32
SLOTS = PLANE * CAP
WCOLS = FEAT + WIDTH
HALF = WCOLS // 2
ROWS = FEAT // NZ
F32, BF16 = jnp.float32, jnp.bfloat16


def erf(v):
    v = jnp.clip(v, -3.832506856900711, 3.832506856900711)
    s = v * v
    top = jnp.float32(0.00022905065861350646)
    for coef in (
        0.0034082910107109506,
        0.050955695062380861,
        0.18520832239976145,
        1.128379143519084,
    ):
        top = top * s + jnp.float32(coef)
    low = jnp.float32(-1.1791602954361697e-7)
    for coef in (
        0.000023547966471313185,
        0.0010179625278914885,
        0.014070470171167667,
        0.11098505178285362,
        0.49746925110067538,
        1.0,
    ):
        low = low * s + jnp.float32(coef)
    return v * top / low


def kernel(
    feat_in, wh_in, wo_in, lists_ref, cent_ref, q_in,
    codes_ref, best_ref,
    feat, wfull, normed, hid, squares, sel, send, recv, slists, glists, onehot, centre, scored, qbuf,
    loc, ws, wz_r, wp_r, wc_r, qs, q1_r, q2_r, qc_r, ls, lr, av, ar,
):
    me = lax.axis_index("lists")
    z = lax.axis_index("refresh")
    y, x, c = me // (NX * NC), (me // NC) % NX, me % NC

    def at(dy, dx, dc):
        return ((y + dy) % NY * NX + (x + dx) % NX) * NC + (c + dc) % NC

    def to(lists, refresh=None):
        return (z if refresh is None else refresh, lists)

    def push(src, dst, send_sem, recv_sem, device):
        pltpu.make_async_remote_copy(
            src_ref=src, dst_ref=dst, send_sem=send_sem, recv_sem=recv_sem,
            device_id=device, device_id_type=MESH,
        ).start()

    def await_bytes(ref, sem):
        pltpu.make_async_copy(ref, ref, sem).wait()

    barrier = pltpu.get_barrier_semaphore()

    def greet_plane(k, _):
        pl.semaphore_signal(
            barrier, inc=1, device_id=to(at(k // 8, (k // 2) % 4, k % 2)), device_id_type=MESH
        )
        return 0

    def greet_z(k, _):
        pl.semaphore_signal(barrier, inc=1, device_id=to(me, (z + k) % NZ), device_id_type=MESH)
        return 0

    lax.fori_loop(1, PLANE, greet_plane, 0)
    lax.fori_loop(1, NZ, greet_z, 0)
    mine = pl.ds(pl.multiple_of(z * ROWS, ROWS), ROWS)
    own = [
        pltpu.make_async_copy(wh_in, wfull.at[mine, pl.ds(0, FEAT)], loc.at[0]),
        pltpu.make_async_copy(wo_in, wfull.at[mine, pl.ds(FEAT, WIDTH)], loc.at[1]),
        pltpu.make_async_copy(q_in, qbuf.at[me], loc.at[2]),
        pltpu.make_async_copy(feat_in, feat, loc.at[3]),
    ]
    for copy in own:
        copy.start()
    for copy in own[:3]:
        copy.wait()
    pl.semaphore_wait(barrier, PLANE - 1 + NZ - 1)

    def piece(plane, half, index):
        row = pl.multiple_of(plane * ROWS + c * (ROWS // 2) + index * 16, 16)
        return wfull.at[pl.ds(row, 16), pl.ds(half * HALF, HALF)]

    def core_part(plane, half, core):
        row = pl.multiple_of(plane * ROWS + core * (ROWS // 2), ROWS // 2)
        return wfull.at[pl.ds(row, ROWS // 2), pl.ds(half * HALF, HALF)]

    def step(i):
        near = i // 2 + 1
        return near + (i % 2) * (NZ - 2 * near)

    def send_z(i, _):
        d = step(i)
        there = to(me, (z + d) % NZ)
        for half, index in ((0, x), (1, y)):
            part = piece(z, half, index)
            push(part, part, ws.at[0], wz_r.at[d - 1, half], there)
        return 0

    lax.fori_loop(0, NZ - 1, send_z, 0)

    def rows(block, half):
        return qbuf.at[block, pl.ds(half * 256, 256)]

    for d in (1, 3, 2):
        push(rows(me, 0), rows(me, 0), qs.at[0], q1_r.at[0, d - 1], to(at(0, d, 0)))
        push(rows(me, 1), rows(me, 1), qs.at[0], q1_r.at[1, d - 1], to(at(d, 0, 0)))
    push(qbuf.at[me], qbuf.at[me], qs.at[2], qc_r.at[0], to(at(0, 0, 1)))

    ids = lists_ref[...]
    owner = lax.shift_right_logical(ids, 7)
    within = ids - owner * LISTS
    table = (lax.broadcasted_iota(jnp.int32, (PLANE, ITEMS), 0) == owner).astype(F32)
    earlier = (
        lax.broadcasted_iota(jnp.int32, (ITEMS, ITEMS), 0)
        < lax.broadcasted_iota(jnp.int32, (ITEMS, ITEMS), 1)
    ).astype(F32)
    prior = jnp.dot(table.astype(BF16), earlier.astype(BF16), preferred_element_type=F32)
    rank = jnp.sum(prior * table, axis=0, keepdims=True).astype(jnp.int32)
    rank_table = (lax.broadcasted_iota(jnp.int32, (128, ITEMS), 0) == rank).astype(F32)
    marked = table * (within + 1).astype(F32)
    slot_lists = lax.dot_general(
        marked.astype(BF16), rank_table.astype(BF16), (((1,), (1,)), ((), ())),
        preferred_element_type=F32,
    )
    slists[...] = slot_lists.reshape(PLANE, 1, 128)

    def send_lists(k, _):
        peer = at(k // 8, (k // 2) % 4, k % 2)
        push(slists.at[peer], glists.at[me], ls, lr, to(peer))
        return 0

    lax.fori_loop(1, PLANE, send_lists, 0)
    glists[me] = slists[me]

    slot = owner * CAP + rank
    for r in range(0, SLOTS, 256):
        sel[r : r + 256, :] = (
            (lax.broadcasted_iota(jnp.int32, (256, ITEMS), 0) + r == slot).astype(F32).astype(BF16)
        )

    own[3].wait()

    def norm_rows(i, _):
        r = pl.ds(pl.multiple_of(i * 64, 64), 64)
        v = feat[r, :].astype(F32)
        scale = lax.rsqrt(jnp.mean(v * v, axis=-1, keepdims=True) + 1e-06)
        normed[r, :] = (v * scale).astype(BF16)
        return 0

    lax.fori_loop(0, ITEMS // 64, norm_rows, 0)

    def spread(i, _):
        d = step(i)
        plane = (z - d + NZ) % NZ
        for half, index in ((0, x), (1, y)):
            part = piece(plane, half, index)
            await_bytes(part, wz_r.at[d - 1, half])
            for e in (1, 3, 2):
                there = to(at(0, e, 0)) if half == 0 else to(at(e, 0, 0))
                push(part, part, ws.at[1], wp_r.at[d - 1, half, e - 1], there)
        return 0

    lax.fori_loop(0, NZ - 1, spread, 0)

    def pair(i, _):
        d = step(i)
        plane = (z - d + NZ) % NZ
        for half, index in ((0, x), (1, y)):
            for e in (1, 3, 2):
                await_bytes(piece(plane, half, (index - e + 4) % 4), wp_r.at[d - 1, half, e - 1])
            part = core_part(plane, half, c)
            push(part, part, ws.at[2], wc_r.at[d - 1, half], to(at(0, 0, 1)))
        return 0

    lax.fori_loop(0, NZ - 1, pair, 0)

    for e in range(4):
        if e:
            await_bytes(rows(at(0, -e + 4, 0), 0), q1_r.at[0, e - 1])
            await_bytes(rows(at(-e + 4, 0, 0), 1), q1_r.at[1, e - 1])
        for d in (1, 3, 2):
            a, b = rows(at(0, 4 - e, 0), 0), rows(at(4 - e, 0, 0), 1)
            push(a, a, qs.at[1], q2_r.at[0, e, d - 1], to(at(d, 0, 0)))
            push(b, b, qs.at[1], q2_r.at[1, e, d - 1], to(at(0, d, 0)))

    def paired(i, _):
        d = step(i)
        plane = (z - d + NZ) % NZ
        for half in range(2):
            await_bytes(core_part(plane, half, 1 - c), wc_r.at[d - 1, half])
        return 0

    lax.fori_loop(0, NZ - 1, paired, 0)

    squares[...] = jnp.zeros_like(squares)

    def hidden(n, _):
        i, j = n % 2, n // 2
        r = pl.ds(pl.multiple_of(i * 256, 256), 256)
        cols = pl.ds(pl.multiple_of(j * 256, 256), 256)
        pre = jnp.dot(normed[r, :], wfull[:, cols], preferred_element_type=F32)
        gelu = 0.5 * pre * (1.0 + erf(pre * 0.7071067811865476))
        h = (feat[r, cols].astype(F32) + gelu).astype(BF16)
        hid[r, cols] = h
        h = h.astype(F32)
        h = h * h
        squares[r, :] += h[:, :128] + h[:, 128:]
        return 0

    lax.fori_loop(0, 8, hidden, 0)

    def vectors(i, _):
        r = pl.ds(pl.multiple_of(i * 128, 128), 128)
        total = jnp.sum(squares[r, :], axis=-1, keepdims=True)
        scale = lax.rsqrt(total * (1.0 / FEAT) + 1e-06)
        hnorm = (hid[r, :].astype(F32) * scale).astype(BF16)
        out = jnp.dot(hnorm, wfull[:, pl.ds(FEAT, WIDTH)], preferred_element_type=F32)
        normed[r, pl.ds(0, WIDTH)] = out.astype(BF16)
        return 0

    lax.fori_loop(0, 4, vectors, 0)

    def fill(i, _):
        r = pl.ds(pl.multiple_of(i * 256, 256), 256)
        out = jnp.dot(sel[r, :], normed[:, pl.ds(0, WIDTH)], preferred_element_type=F32)
        send[pl.ds(i * 8, 8)] = out.astype(BF16).reshape(8, CAP, WIDTH)
        return 0

    lax.fori_loop(0, 4, fill, 0)

    def route(k, _):
        peer = at(k // 8, (k // 2) % 4, k % 2)
        push(send.at[peer], recv.at[me], av, ar, to(peer))
        return 0

    lax.fori_loop(1, PLANE, route, 0)
    recv[me] = send[me]

    await_bytes(glists.at[pl.ds(0, PLANE - 1)], lr)
    marks = jnp.transpose(glists[...].reshape(PLANE, 128))
    lane = lax.broadcasted_iota(jnp.int32, (CAP, LISTS), 1).astype(F32) + 1.0
    for s in range(PLANE):
        column = marks[:CAP, s : s + 1]
        onehot[s * CAP : (s + 1) * CAP, :] = (column == lane).astype(F32).astype(BF16)
    centre[...] = jnp.dot(onehot[...], cent_ref[...], preferred_element_type=F32)
    filled = jnp.sum(onehot[...].astype(F32), axis=1, keepdims=True) > 0.5
    places = lax.broadcasted_iota(jnp.int32, (SLOTS, 1), 0).astype(F32)
    first = jnp.min(jnp.where(filled, places, 2.0 * SLOTS), axis=0, keepdims=True)
    some = first < SLOTS

    await_bytes(recv.at[pl.ds(0, PLANE - 1)], ar)
    codes = (recv[...].reshape(SLOTS, WIDTH).astype(F32) - centre[...]).astype(BF16)
    codes_ref[...] = codes
    codes = codes.astype(F32)
    spare = jnp.sum(jnp.where(places == first, codes, 0.0), axis=0, keepdims=True)
    scored[...] = jnp.where(filled, codes, spare).astype(BF16)

    def score(block):
        top = None
        for r in range(0, SLOTS, 256):
            s = lax.dot_general(
                scored[r : r + 256, :], qbuf[block], (((1,), (1,)), ((), ())),
                preferred_element_type=F32,
            )
            s = jnp.max(s.reshape(32, 8, 512), axis=0)
            top = s if top is None else jnp.maximum(top, s)
        top = jnp.max(top, axis=0, keepdims=True)
        best_ref[:, pl.ds(pl.multiple_of(block * 512, 512), 512)] = jnp.where(some, top, -1e30)

    score(me)
    await_bytes(qbuf.at[0], qc_r.at[0])
    score(at(0, 0, 1))

    for k in range(1, 16):
        dy, dx = k // 4, k % 4
        block = at(4 - dy, 4 - dx, 0)
        if dy > 0:
            await_bytes(rows(block, 0), q2_r.at[0, dx, dy - 1])
        if dx > 0:
            await_bytes(rows(block, 1), q2_r.at[1, dy, dx - 1])
        push(qbuf.at[block], qbuf.at[block], qs.at[2], qc_r.at[k], to(at(0, 0, 1)))

    def rest(k, _):
        dy, dx = k // 4, k % 4
        score(at(4 - dy, 4 - dx, 0))
        block = at(4 - dy, 4 - dx, 1)
        await_bytes(qbuf.at[block], qc_r.at[k])
        score(block)
        return 0

    lax.fori_loop(1, 16, rest, 0)

    await_bytes(wfull.at[pl.ds(0, 112)], ws.at[0])
    await_bytes(wfull.at[pl.ds(0, 336)], ws.at[1])
    await_bytes(wfull.at[pl.ds(0, 448)], ws.at[2])
    await_bytes(qbuf.at[pl.ds(0, 3)], qs.at[0])
    await_bytes(qbuf.at[pl.ds(0, 12)], qs.at[1])
    await_bytes(qbuf.at[pl.ds(0, 16)], qs.at[2])
    await_bytes(slists.at[pl.ds(0, PLANE - 1)], ls)
    await_bytes(send.at[pl.ds(0, PLANE - 1)], av)


def per_device(features, w_hidden, w_out, list_ids, centroids, queries):
    anywhere, vmem = pl.BlockSpec(memory_space=pl.ANY), pl.BlockSpec(memory_space=pltpu.VMEM)
    dma = pltpu.SemaphoreType.DMA
    return pl.pallas_call(
        kernel,
        out_shape=(
            jax.ShapeDtypeStruct((SLOTS, WIDTH), BF16),
            jax.ShapeDtypeStruct((1, PLANE * ITEMS), F32),
        ),
        in_specs=[anywhere, anywhere, anywhere, vmem, vmem, anywhere],
        out_specs=(vmem, vmem),
        scratch_shapes=[
            pltpu.VMEM((ITEMS, FEAT), BF16),
            pltpu.VMEM((FEAT, WCOLS), BF16),
            pltpu.VMEM((ITEMS, FEAT), BF16),
            pltpu.VMEM((ITEMS, FEAT), BF16),
            pltpu.VMEM((ITEMS, 128), F32),
            pltpu.VMEM((SLOTS, ITEMS), BF16),
            pltpu.VMEM((PLANE, CAP, WIDTH), BF16),
            pltpu.VMEM((PLANE, CAP, WIDTH), BF16),
            pltpu.VMEM((PLANE, 1, 128), F32),
            pltpu.VMEM((PLANE, 1, 128), F32),
            pltpu.VMEM((SLOTS, LISTS), BF16),
            pltpu.VMEM((SLOTS, WIDTH), F32),
            pltpu.VMEM((SLOTS, WIDTH), BF16),
            pltpu.VMEM((PLANE, ITEMS, WIDTH), BF16),
            dma((4,)), dma((3,)), dma((7, 2)), dma((7, 2, 3)), dma((7, 2)),
            dma((3,)), dma((2, 3)), dma((2, 4, 3)), dma((16,)),
            dma, dma, dma, dma,
        ],
        compiler_params=pltpu.CompilerParams(
            collective_id=0, has_side_effects=True, vmem_limit_bytes=50 * 2**20
        ),
        name="refresh",
    )(features, w_hidden, w_out, list_ids.reshape(1, ITEMS), centroids, queries)


def solution(mesh):
    in_specs = (
        P(("refresh", "lists"), None),
        P("refresh", None),
        P("refresh", None),
        P(("refresh", "lists")),
        P("lists", None),
        P("lists", None),
    )
    out_specs = (P(("refresh", "lists"), None), P(("refresh", "lists"), None))
    return jax.shard_map(
        per_device, mesh=mesh, in_specs=in_specs, out_specs=out_specs, check_vma=False
    )
```

```python
import jax
import jax.numpy as jnp
from jax import lax
from jax.experimental import pallas as pl
from jax.experimental.pallas import tpu as pltpu
from jax.sharding import PartitionSpec as P

MESH = pl.DeviceIdType.MESH
NY, NX, NC, NZ = 4, 4, 2, 8
PLANE = NY * NX * NC
ITEMS, FEAT, WIDTH, LISTS, CAP = 512, 1024, 256, 128, 32
SLOTS = PLANE * CAP
WCOLS = FEAT + WIDTH
HALF = WCOLS // 2
ROWS = FEAT // NZ
F32, BF16 = jnp.float32, jnp.bfloat16


def erf(v):
    v = jnp.clip(v, -3.832506856900711, 3.832506856900711)
    s = v * v
    top = jnp.float32(0.00022905065861350646)
    for coef in (
        0.0034082910107109506,
        0.050955695062380861,
        0.18520832239976145,
        1.128379143519084,
    ):
        top = top * s + jnp.float32(coef)
    low = jnp.float32(-1.1791602954361697e-7)
    for coef in (
        0.000023547966471313185,
        0.0010179625278914885,
        0.014070470171167667,
        0.11098505178285362,
        0.49746925110067538,
        1.0,
    ):
        low = low * s + jnp.float32(coef)
    return v * top / low


def kernel(
    feat_in, wh_in, wo_in, lists_in, cent_in, q_in,
    recv, q_out, centre_out, place_out, count_out,
    feat, wfull, normed, hid, squares, sel, send, ids_ref, cent, slists, glists, onehot, centre, place, count,
    loc, ws, wz_r, wp_r, wc_r, qs, q1_r, q2_r, qc_r, ls, lr, av, ar,
):
    me = lax.axis_index("lists")
    z = lax.axis_index("refresh")
    y, x, c = me // (NX * NC), (me // NC) % NX, me % NC

    def at(dy, dx, dc):
        return ((y + dy) % NY * NX + (x + dx) % NX) * NC + (c + dc) % NC

    def to(lists, refresh=None):
        return (z if refresh is None else refresh, lists)

    def push(src, dst, send_sem, recv_sem, device):
        pltpu.make_async_remote_copy(
            src_ref=src, dst_ref=dst, send_sem=send_sem, recv_sem=recv_sem,
            device_id=device, device_id_type=MESH,
        ).start()

    def await_bytes(ref, sem):
        pltpu.make_async_copy(ref, ref, sem).wait()

    barrier = pltpu.get_barrier_semaphore()

    def greet_plane(k, _):
        pl.semaphore_signal(
            barrier, inc=1, device_id=to(at(k // 8, (k // 2) % 4, k % 2)), device_id_type=MESH
        )
        return 0

    def greet_z(k, _):
        pl.semaphore_signal(barrier, inc=1, device_id=to(me, (z + k) % NZ), device_id_type=MESH)
        return 0

    lax.fori_loop(1, PLANE, greet_plane, 0)
    lax.fori_loop(1, NZ, greet_z, 0)
    mine = pl.ds(pl.multiple_of(z * ROWS, ROWS), ROWS)
    own = [
        pltpu.make_async_copy(wh_in, wfull.at[mine, pl.ds(0, FEAT)], loc.at[0]),
        pltpu.make_async_copy(wo_in, wfull.at[mine, pl.ds(FEAT, WIDTH)], loc.at[1]),
        pltpu.make_async_copy(lists_in, ids_ref, loc.at[2]),
        pltpu.make_async_copy(feat_in, feat, loc.at[3]),
        pltpu.make_async_copy(cent_in, cent, loc.at[4]),
        pltpu.make_async_copy(q_in, q_out.at[me], loc.at[5]),
    ]
    for copy in own:
        copy.start()
    for copy in own[:3]:
        copy.wait()
    pl.semaphore_wait(barrier, PLANE - 1 + NZ - 1)

    def piece(plane, half, index):
        row = pl.multiple_of(plane * ROWS + c * (ROWS // 2) + index * 16, 16)
        return wfull.at[pl.ds(row, 16), pl.ds(half * HALF, HALF)]

    def core_part(plane, half, core):
        row = pl.multiple_of(plane * ROWS + core * (ROWS // 2), ROWS // 2)
        return wfull.at[pl.ds(row, ROWS // 2), pl.ds(half * HALF, HALF)]

    def step(i):
        near = i // 2 + 1
        return near + (i % 2) * (NZ - 2 * near)

    def send_z(i, _):
        d = step(i)
        there = to(me, (z + d) % NZ)
        for half, index in ((0, x), (1, y)):
            part = piece(z, half, index)
            push(part, part, ws.at[0], wz_r.at[d - 1, half], there)
        return 0

    lax.fori_loop(0, NZ - 1, send_z, 0)

    def rows(block, half):
        return q_out.at[block, pl.ds(half * 256, 256)]

    def own_rows(half):
        return q_in.at[pl.ds(half * 256, 256)]

    def over(half, d):
        return to(at(0, d, 0)) if half == 0 else to(at(d, 0, 0))

    def first_leg(half, d):
        push(own_rows(half), rows(me, half), qs.at[0], q1_r.at[half, d - 1], over(half, d))

    def second_leg(half, e, d):
        block = at(0, 4 - e, 0) if half == 0 else at(4 - e, 0, 0)
        src = rows(block, half) if e else own_rows(half)
        push(src, rows(block, half), qs.at[1], q2_r.at[half, e, d - 1], over(1 - half, d))

    def arrived(half, e, d):
        block = at(4 - d, 4 - e, 0) if half == 0 else at(4 - e, 4 - d, 0)
        await_bytes(rows(block, half), q2_r.at[half, e, d - 1])
        return block

    def pass_on(half, e, d):
        block = arrived(half, e, d)
        push(rows(block, half), rows(block, half), qs.at[1], q2_r.at[half, e, 1], over(1 - half, d))

    for half in range(2):
        for d in (1, 3):
            first_leg(half, d)
    for half in range(2):
        second_leg(half, 0, 1)
        first_leg(half, 2)
        second_leg(half, 0, 3)
    push(q_in, q_out.at[me], qs.at[2], qc_r.at[0], to(at(0, 0, 1)))

    ids = ids_ref[...]
    owner = lax.shift_right_logical(ids, 7)
    within = ids - owner * LISTS
    table = (lax.broadcasted_iota(jnp.int32, (PLANE, ITEMS), 0) == owner).astype(F32)
    earlier = (
        lax.broadcasted_iota(jnp.int32, (ITEMS, ITEMS), 0)
        < lax.broadcasted_iota(jnp.int32, (ITEMS, ITEMS), 1)
    ).astype(F32)
    prior = jnp.dot(table.astype(BF16), earlier.astype(BF16), preferred_element_type=F32)
    rank = jnp.sum(prior * table, axis=0, keepdims=True).astype(jnp.int32)
    rank_table = (lax.broadcasted_iota(jnp.int32, (128, ITEMS), 0) == rank).astype(F32)
    marked = table * (within + 1).astype(F32)
    slot_lists = lax.dot_general(
        marked.astype(BF16), rank_table.astype(BF16), (((1,), (1,)), ((), ())),
        preferred_element_type=F32,
    )
    slists[...] = slot_lists.reshape(PLANE, 1, 128)

    def send_lists(k, _):
        peer = at(k // 8, (k // 2) % 4, k % 2)
        push(slists.at[peer], glists.at[me], ls, lr, to(peer))
        return 0

    lax.fori_loop(1, PLANE, send_lists, 0)
    glists[me] = slists[me]

    slot = owner * CAP + rank
    for r in range(0, SLOTS, 256):
        sel[r : r + 256, :] = (
            (lax.broadcasted_iota(jnp.int32, (256, ITEMS), 0) + r == slot).astype(F32).astype(BF16)
        )

    own[3].wait()

    def norm_rows(i, _):
        r = pl.ds(pl.multiple_of(i * 64, 64), 64)
        v = feat[r, :].astype(F32)
        scale = lax.rsqrt(jnp.mean(v * v, axis=-1, keepdims=True) + 1e-06)
        normed[r, :] = (v * scale).astype(BF16)
        return 0

    lax.fori_loop(0, ITEMS // 64, norm_rows, 0)

    def spread(i, _):
        d = step(i)
        plane = (z - d + NZ) % NZ
        for half, index in ((0, x), (1, y)):
            part = piece(plane, half, index)
            await_bytes(part, wz_r.at[d - 1, half])
            for e in (1, 3, 2):
                there = to(at(0, e, 0)) if half == 0 else to(at(e, 0, 0))
                push(part, part, ws.at[1], wp_r.at[d - 1, half, e - 1], there)
        return 0

    lax.fori_loop(0, NZ - 1, spread, 0)

    for e, d in ((1, 1), (3, 3), (2, 3), (1, 3), (3, 1), (2, 1)):
        for half in range(2):
            if (e, d) in ((1, 1), (3, 3), (2, 3)):
                block = at(0, 4 - e, 0) if half == 0 else at(4 - e, 0, 0)
                await_bytes(rows(block, half), q1_r.at[half, e - 1])
            second_leg(half, e, d)
    for half in range(2):
        pass_on(half, 0, 1)

    def pair(i, _):
        d = step(i)
        plane = (z - d + NZ) % NZ
        for half, index in ((0, x), (1, y)):
            for e in (1, 3, 2):
                await_bytes(piece(plane, half, (index - e + 4) % 4), wp_r.at[d - 1, half, e - 1])
            part = core_part(plane, half, c)
            push(part, part, ws.at[2], wc_r.at[d - 1, half], to(at(0, 0, 1)))
        return 0

    lax.fori_loop(0, NZ - 1, pair, 0)

    own[4].wait()
    await_bytes(glists.at[pl.ds(0, PLANE - 1)], lr)
    marks = jnp.transpose(glists[...].reshape(PLANE, 128))
    lane = lax.broadcasted_iota(jnp.int32, (CAP, LISTS), 1).astype(F32) + 1.0
    for s in range(PLANE):
        column = marks[:CAP, s : s + 1]
        onehot[s * CAP : (s + 1) * CAP, :] = (column == lane).astype(F32).astype(BF16)
    centre[...] = jnp.dot(onehot[...], cent[...], preferred_element_type=F32).astype(BF16)
    held = jnp.sum((marks > 0.5).astype(F32), axis=0, keepdims=True)
    below = (
        lax.broadcasted_iota(jnp.int32, (PLANE, PLANE), 0)
        < lax.broadcasted_iota(jnp.int32, (PLANE, PLANE), 1)
    ).astype(F32)
    start = jnp.dot(held.astype(BF16), below.astype(BF16), preferred_element_type=F32)
    high = jnp.floor(start * (1.0 / CAP))
    low = start - high * CAP
    source = lax.shift_right_logical(lax.broadcasted_iota(jnp.int32, (PLANE, SLOTS), 1), 5)
    member = (lax.broadcasted_iota(jnp.int32, (PLANE, SLOTS), 0) == source).astype(F32).astype(BF16)

    def spread_out(row):
        return jnp.dot(row.astype(BF16), member, preferred_element_type=F32)

    within_source = (lax.broadcasted_iota(jnp.int32, (1, SLOTS), 1) & (CAP - 1)).astype(F32)
    place[...] = jnp.where(
        within_source < spread_out(held),
        spread_out(high) * CAP + spread_out(low) + within_source,
        -1.0,
    )
    count[...] = jnp.broadcast_to(jnp.sum(held, axis=1, keepdims=True), (1, 128)).astype(jnp.int32)
    results = [
        pltpu.make_async_copy(centre, centre_out, loc.at[6]),
        pltpu.make_async_copy(place, place_out, loc.at[7]),
        pltpu.make_async_copy(count, count_out, loc.at[8]),
    ]
    for copy in results:
        copy.start()

    def paired(i, _):
        d = step(i)
        plane = (z - d + NZ) % NZ
        for half in range(2):
            await_bytes(core_part(plane, half, 1 - c), wc_r.at[d - 1, half])
        return 0

    lax.fori_loop(0, NZ - 1, paired, 0)

    squares[...] = jnp.zeros_like(squares)

    def hidden(n, _):
        i, j = n % 2, n // 2
        r = pl.ds(pl.multiple_of(i * 256, 256), 256)
        cols = pl.ds(pl.multiple_of(j * 256, 256), 256)
        pre = jnp.dot(normed[r, :], wfull[:, cols], preferred_element_type=F32)
        gelu = 0.5 * pre * (1.0 + erf(pre * 0.7071067811865476))
        h = (feat[r, cols].astype(F32) + gelu).astype(BF16)
        hid[r, cols] = h
        h = h.astype(F32)
        h = h * h
        squares[r, :] += h[:, :128] + h[:, 128:]
        return 0

    lax.fori_loop(0, 8, hidden, 0)

    for e, d in ((1, 1), (3, 3), (2, 3)):
        for half in range(2):
            pass_on(half, e, d)

    def vectors(i, _):
        r = pl.ds(pl.multiple_of(i * 128, 128), 128)
        total = jnp.sum(squares[r, :], axis=-1, keepdims=True)
        scale = lax.rsqrt(total * (1.0 / FEAT) + 1e-06)
        hnorm = (hid[r, :].astype(F32) * scale).astype(BF16)
        out = jnp.dot(hnorm, wfull[:, pl.ds(FEAT, WIDTH)], preferred_element_type=F32)
        normed[r, pl.ds(0, WIDTH)] = out.astype(BF16)
        return 0

    lax.fori_loop(0, 4, vectors, 0)

    def fill(i, _):
        r = pl.ds(pl.multiple_of(i * 256, 256), 256)
        out = jnp.dot(sel[r, :], normed[:, pl.ds(0, WIDTH)], preferred_element_type=F32)
        send[pl.ds(i * 8, 8)] = out.astype(BF16).reshape(8, CAP, WIDTH)
        return 0

    lax.fori_loop(0, 4, fill, 0)

    def route(k, _):
        peer = at(k // 8, (k // 2) % 4, k % 2)
        push(send.at[peer], recv.at[me], av, ar, to(peer))
        return 0

    lax.fori_loop(1, PLANE, route, 0)
    keep = pltpu.make_async_copy(send.at[me], recv.at[me], loc.at[9])
    keep.start()

    own[5].wait()
    for dy, dx in sorted(
        ((k // 4, k % 4) for k in range(1, 16)), key=lambda p: (p[0] == 2) + (p[1] == 2)
    ):
        block = at(4 - dy, 4 - dx, 0)
        if dy > 0 and not (dx in (0, 1) and dy == 1 or dx in (2, 3) and dy == 3):
            arrived(0, dx, dy)
        if dx > 0 and not (dy in (0, 1) and dx == 1 or dy in (2, 3) and dx == 3):
            arrived(1, dy, dx)
        push(q_out.at[block], q_out.at[block], qs.at[2], qc_r.at[dy * 4 + dx], to(at(0, 0, 1)))
    for k in range(16):
        await_bytes(q_out.at[at(4 - k // 4, 4 - k % 4, 1)], qc_r.at[k])
    await_bytes(recv.at[pl.ds(0, PLANE - 1)], ar)

    await_bytes(wfull.at[pl.ds(0, 112)], ws.at[0])
    await_bytes(wfull.at[pl.ds(0, 336)], ws.at[1])
    await_bytes(wfull.at[pl.ds(0, 448)], ws.at[2])
    await_bytes(q_out.at[pl.ds(0, 3)], qs.at[0])
    await_bytes(q_out.at[pl.ds(0, 12)], qs.at[1])
    await_bytes(q_out.at[pl.ds(0, 16)], qs.at[2])
    await_bytes(slists.at[pl.ds(0, PLANE - 1)], ls)
    await_bytes(send.at[pl.ds(0, PLANE - 1)], av)
    keep.wait()
    for copy in results:
        copy.wait()


VARIANTS = (256, 512, 576, 640, 704, 768, 1024)
TILE = 4096


def score_kernel(count_ref, recv_ref, centre_ref, place_ref, q_ref, codes_ref, best_ref, packed):
    count = count_ref[0, 0]

    @pl.when(pl.program_id(0) == 0)
    def _():
        codes = (recv_ref[...].astype(F32) - centre_ref[...].astype(F32)).astype(BF16)
        codes_ref[...] = codes
        last = jnp.maximum(count - 1, 0)
        for r in range(0, SLOTS, 128):

            @pl.when((r == 0) | (r < count + 127))
            def _():
                row = jnp.minimum(lax.broadcasted_iota(jnp.int32, (128, SLOTS), 0) + r, last)
                pick = (row.astype(F32) == place_ref[...]).astype(F32).astype(BF16)
                packed[r : r + 128, :] = jnp.dot(
                    pick, codes, preferred_element_type=F32
                ).astype(BF16)

    for at, size in enumerate(VARIANTS):
        less = VARIANTS[at - 1] if at else -1

        @pl.when((count > less) & (count <= size))
        def _():
            for lo in range(0, TILE, 256):
                s = lax.dot_general(
                    packed[:size, :], q_ref[lo : lo + 256, :], (((1,), (1,)), ((), ())),
                    preferred_element_type=F32,
                )
                best_ref[:, lo : lo + 256] = jnp.max(s, axis=0, keepdims=True)

    @pl.when(count == 0)
    def _():
        best_ref[...] = jnp.full_like(best_ref, -1e30)


def per_device(features, w_hidden, w_out, list_ids, centroids, queries):
    anywhere = pl.BlockSpec(memory_space=pl.ANY)
    dma = pltpu.SemaphoreType.DMA
    recv, q_all, centre, place, count = pl.pallas_call(
        kernel,
        out_shape=(
            jax.ShapeDtypeStruct((PLANE, CAP, WIDTH), BF16),
            jax.ShapeDtypeStruct((PLANE, ITEMS, WIDTH), BF16),
            jax.ShapeDtypeStruct((SLOTS, WIDTH), BF16),
            jax.ShapeDtypeStruct((1, SLOTS), F32),
            jax.ShapeDtypeStruct((1, 128), jnp.int32),
        ),
        in_specs=[anywhere] * 6,
        out_specs=(anywhere,) * 5,
        scratch_shapes=[
            pltpu.VMEM((ITEMS, FEAT), BF16),
            pltpu.VMEM((FEAT, WCOLS), BF16),
            pltpu.VMEM((ITEMS, FEAT), BF16),
            pltpu.VMEM((ITEMS, FEAT), BF16),
            pltpu.VMEM((ITEMS, 128), F32),
            pltpu.VMEM((SLOTS, ITEMS), BF16),
            pltpu.VMEM((PLANE, CAP, WIDTH), BF16),
            pltpu.VMEM((1, ITEMS), jnp.int32),
            pltpu.VMEM((LISTS, WIDTH), BF16),
            pltpu.VMEM((PLANE, 1, 128), F32),
            pltpu.VMEM((PLANE, 1, 128), F32),
            pltpu.VMEM((SLOTS, LISTS), BF16),
            pltpu.VMEM((SLOTS, WIDTH), BF16),
            pltpu.VMEM((1, SLOTS), F32),
            pltpu.VMEM((1, 128), jnp.int32),
            dma((10,)), dma((3,)), dma((7, 2)), dma((7, 2, 3)), dma((7, 2)),
            dma((3,)), dma((2, 3)), dma((2, 4, 3)), dma((16,)),
            dma, dma, dma, dma,
        ],
        compiler_params=pltpu.CompilerParams(
            collective_id=0, has_side_effects=True, vmem_limit_bytes=62 * 2**20
        ),
        name="encode_and_route",
    )(features, w_hidden, w_out, list_ids.reshape(1, ITEMS), centroids, queries)
    whole = lambda *shape: pl.BlockSpec(shape, lambda i: (0,) * len(shape))
    return pl.pallas_call(
        score_kernel,
        grid=(PLANE * ITEMS // TILE,),
        out_shape=(
            jax.ShapeDtypeStruct((SLOTS, WIDTH), BF16),
            jax.ShapeDtypeStruct((1, PLANE * ITEMS), F32),
        ),
        in_specs=[
            pl.BlockSpec(memory_space=pltpu.SMEM),
            whole(SLOTS, WIDTH),
            whole(SLOTS, WIDTH),
            whole(1, SLOTS),
            pl.BlockSpec((TILE, WIDTH), lambda i: (i, 0)),
        ],
        out_specs=(whole(SLOTS, WIDTH), pl.BlockSpec((1, TILE), lambda i: (0, i))),
        scratch_shapes=[pltpu.VMEM((SLOTS, WIDTH), BF16)],
        compiler_params=pltpu.CompilerParams(vmem_limit_bytes=60 * 2**20),
        name="score",
    )(
        count,
        recv.reshape(SLOTS, WIDTH),
        centre,
        place,
        q_all.reshape(PLANE * ITEMS, WIDTH),
    )


def solution(mesh):
    in_specs = (
        P(("refresh", "lists"), None),
        P("refresh", None),
        P("refresh", None),
        P(("refresh", "lists")),
        P("lists", None),
        P("lists", None),
    )
    out_specs = (P(("refresh", "lists"), None), P(("refresh", "lists"), None))
    return jax.shard_map(
        per_device, mesh=mesh, in_specs=in_specs, out_specs=out_specs, check_vma=False
    )
```

```python
import jax
import jax.numpy as jnp
from jax import lax
from jax.experimental import pallas as pl
from jax.experimental.pallas import tpu as pltpu
from jax.sharding import PartitionSpec as P

MESH = pl.DeviceIdType.MESH
NY, NX, NC, NZ = 4, 4, 2, 8
PLANE = NY * NX * NC
ITEMS, FEAT, WIDTH, LISTS, CAP = 512, 1024, 256, 128, 32
SLOTS = PLANE * CAP
WCOLS = FEAT + WIDTH
STAGES = ((0, 512), (512, 512), (1024, 256))
ROWS = FEAT // NZ
PART = ITEMS // 2
F32, BF16 = jnp.float32, jnp.bfloat16


def kernel(
    feat_in, wh_in, wo_in, lists_in, cent_in, q_in,
    codes_out, packed_out, q_out, count_out,
    feat, wfull, normed, hid, squares, sel, send, recv, ids_ref, cent, slists, glists, onehot,
    codes, pick, packed, count,
    loc, ws, wz_r, wc_r, qs, q1_r, q2_r, qc_r, ls, lr, av, ar,
):
    me = lax.axis_index("lists")
    z = lax.axis_index("refresh")
    y, x, c = me // (NX * NC), (me // NC) % NX, me % NC

    def at(dy, dx, dc):
        return ((y + dy) % NY * NX + (x + dx) % NX) * NC + (c + dc) % NC

    def to(lists, refresh=None):
        return (z if refresh is None else refresh, lists)

    def push(src, dst, send_sem, recv_sem, device):
        pltpu.make_async_remote_copy(
            src_ref=src, dst_ref=dst, send_sem=send_sem, recv_sem=recv_sem,
            device_id=device, device_id_type=MESH,
        ).start()

    def await_bytes(ref, sem):
        pltpu.make_async_copy(ref, ref, sem).wait()

    def each(low, high, body):
        def step_once(i, _):
            body(i)
            return 0

        lax.fori_loop(low, high, step_once, 0)

    other = to(at(0, 0, 1))

    barrier = pltpu.get_barrier_semaphore()

    def peer_of(k):
        return at(k // 8, (k // 2) % 4, k % 2)

    def greet(device):
        pl.semaphore_signal(barrier, inc=1, device_id=device, device_id_type=MESH)

    each(1, PLANE, lambda k: greet(to(peer_of(k))))
    each(1, NZ, lambda k: greet(to(me, (z + k) % NZ)))
    mine = pl.ds(pl.multiple_of(z * ROWS, ROWS), ROWS)
    q_mine = pl.ds(pl.multiple_of(me * ITEMS, ITEMS), ITEMS)
    own = [
        pltpu.make_async_copy(wh_in, wfull.at[mine, pl.ds(0, FEAT)], loc.at[0]),
        pltpu.make_async_copy(wo_in, wfull.at[mine, pl.ds(FEAT, WIDTH)], loc.at[1]),
        pltpu.make_async_copy(lists_in, ids_ref, loc.at[2]),
        pltpu.make_async_copy(feat_in, feat, loc.at[3]),
        pltpu.make_async_copy(cent_in, cent, loc.at[4]),
        pltpu.make_async_copy(q_in, q_out.at[q_mine], loc.at[5]),
    ]
    for copy in own:
        copy.start()
    for copy in own[:3]:
        copy.wait()
    pl.semaphore_wait(barrier, PLANE - 1 + NZ - 1)

    def shard(stage, plane, core, part=None):
        first, width = STAGES[stage]
        if part is not None:
            width //= 2
            first += part * width
        row = pl.multiple_of(plane * ROWS + core * (ROWS // 2), ROWS // 2)
        return wfull.at[pl.ds(row, ROWS // 2), pl.ds(first, width)]

    def source(hop, way):
        return (z + NZ - hop) % NZ if way == 0 else (z + hop) % NZ

    def pass_z(hop, stage, way):
        part = shard(stage, source(hop - 1, way), c, way if hop == 4 else None)
        there = to(me, (z + 1) % NZ if way == 0 else (z + NZ - 1) % NZ)
        push(part, part, ws.at[0], wz_r.at[hop - 1, stage, way], there)

    def land_z(hop, stage):
        for way in range(2):
            part = shard(stage, source(hop, way), c, way if hop == 4 else None)
            await_bytes(part, wz_r.at[hop - 1, stage, way])
            if hop < 4:
                pass_z(hop + 1, stage, way)
        for way in range(2):
            part = shard(stage, source(hop, way), c, way if hop == 4 else None)
            push(part, part, ws.at[1], wc_r.at[hop - 1, stage, way], other)

    def paired(stage):
        for hop in range(1, 5):
            for way in range(2):
                part = shard(stage, source(hop, way), 1 - c, way if hop == 4 else None)
                await_bytes(part, wc_r.at[hop - 1, stage, way])

    def rows(block, first, size):
        return q_out.at[pl.ds(pl.multiple_of(block * ITEMS + first, 64), size)]

    def half_rows(block, half):
        return rows(block, half * PART, PART)

    def own_rows(half):
        return q_in.at[pl.ds(half * PART, PART)]

    def over(half, d):
        return to(at(d * half, d * (1 - half), 0))

    def block_of(half, e, d):
        return at(4 - d - half * (e - d), 4 - e - half * (d - e), 0)

    def first_leg(half, d):
        push(own_rows(half), half_rows(me, half), qs.at[0], q1_r.at[half, d - 1], over(half, d))

    def second_leg(half, e, d):
        here = half_rows(block_of(half, e, 0), half)
        src = here if e else own_rows(half)
        push(src, here, qs.at[1], q2_r.at[half, e, d - 1], over(1 - half, d))

    def share(half, e, d):
        here = half_rows(block_of(half, e, d), half)
        push(here, here, qs.at[2], qc_r.at[half, e, d], other)

    def land_first(e):
        for half in range(2):
            await_bytes(half_rows(me, half), q1_r.at[half, e - 1])
            share(half, e, 0)
            second_leg(half, e, 1)
            second_leg(half, e, 3)

    def land_second(e, d):
        for half in range(2):
            here = half_rows(block_of(half, e, d), half)
            await_bytes(here, q2_r.at[half, e, d - 1])
            if d == (1 if e < 2 else 3):
                push(here, here, qs.at[1], q2_r.at[half, e, 1], over(1 - half, d))
            share(half, e, d)

    for stage in range(3):
        pass_z(1, stage, 0)
        pass_z(1, stage, 1)
    for d in (1, 3, 2):
        for half in range(2):
            first_leg(half, d)
    for d in (1, 3):
        for half in range(2):
            second_leg(half, 0, d)
    for half in range(2):
        push(own_rows(half), half_rows(me, half), qs.at[2], qc_r.at[half, 0, 0], other)

    ids = ids_ref[...]
    owner = lax.shift_right_logical(ids, 7)
    within = ids - owner * LISTS
    table = (lax.broadcasted_iota(jnp.int32, (PLANE, ITEMS), 0) == owner).astype(F32)
    earlier = (
        lax.broadcasted_iota(jnp.int32, (ITEMS, ITEMS), 0)
        < lax.broadcasted_iota(jnp.int32, (ITEMS, ITEMS), 1)
    ).astype(F32)
    prior = jnp.dot(table.astype(BF16), earlier.astype(BF16), preferred_element_type=F32)
    rank = jnp.sum(prior * table, axis=0, keepdims=True).astype(jnp.int32)
    rank_table = (lax.broadcasted_iota(jnp.int32, (128, ITEMS), 0) == rank).astype(F32)
    marked = table * (within + 1).astype(F32)
    slot_lists = lax.dot_general(
        marked.astype(BF16), rank_table.astype(BF16), (((1,), (1,)), ((), ())),
        preferred_element_type=F32,
    )
    slists[...] = slot_lists.reshape(PLANE, 1, 128)
    each(1, PLANE, lambda k: push(slists.at[peer_of(k)], glists.at[me], ls, lr, to(peer_of(k))))
    glists[me] = slists[me]

    own[3].wait()

    def norm_rows(i):
        r = pl.ds(pl.multiple_of(i * 64, 64), 64)
        v = feat[r, :].astype(F32)
        scale = lax.rsqrt(jnp.mean(v * v, axis=-1, keepdims=True) + 1e-06)
        normed[r, :] = (v * scale).astype(BF16)

    each(0, ITEMS // 64, norm_rows)

    for stage in range(3):
        land_z(1, stage)
    land_first(1)
    land_first(3)
    slot = owner * CAP + rank
    for r in range(0, SLOTS, 256):
        sel[r : r + 256, :] = (
            (lax.broadcasted_iota(jnp.int32, (256, ITEMS), 0) + r == slot).astype(F32).astype(BF16)
        )
    for stage in range(3):
        land_z(2, stage)
    land_first(2)
    for stage in range(3):
        land_z(3, stage)
    land_second(0, 1)
    land_second(0, 3)

    squares[...] = jnp.zeros_like(squares)

    def hidden(j):
        cols = pl.ds(pl.multiple_of(j * 256, 256), 256)
        pre = jnp.dot(normed[...], wfull[:, cols], preferred_element_type=F32)
        gelu = 0.5 * pre * (1.0 + lax.erf(pre * 0.7071067811865476))
        h = (feat[:, cols].astype(F32) + gelu).astype(BF16)
        hid[:, cols] = h
        h = h.astype(F32)
        h = h * h
        squares[...] += h[:, :128] + h[:, 128:]

    land_z(4, 0)
    paired(0)
    each(0, 2, hidden)
    land_z(4, 1)
    land_z(4, 2)
    paired(1)
    each(2, 4, hidden)
    paired(2)
    land_second(1, 1)
    land_second(3, 3)
    total = jnp.sum(squares[...], axis=-1, keepdims=True)
    scale = lax.rsqrt(total * (1.0 / FEAT) + 1e-06)
    out = jnp.dot(hid[...], wfull[:, FEAT:], preferred_element_type=F32)
    normed[:, :WIDTH] = (out * scale).astype(BF16)
    for i in range(4):
        out = jnp.dot(
            sel[i * 256 : (i + 1) * 256, :], normed[:, :WIDTH], preferred_element_type=F32
        )
        send[i * 8 : (i + 1) * 8] = out.astype(BF16).reshape(8, CAP, WIDTH)

    each(1, PLANE, lambda k: push(send.at[peer_of(k)], recv.at[me], av, ar, to(peer_of(k))))
    recv[me] = send[me]
    for e, d in ((2, 3), (1, 3), (3, 1), (2, 1)):
        land_second(e, d)

    own[4].wait()
    await_bytes(glists.at[pl.ds(0, PLANE - 1)], lr)
    marks = jnp.transpose(glists[...].reshape(PLANE, 128))
    lane = lax.broadcasted_iota(jnp.int32, (CAP, LISTS), 1).astype(F32) + 1.0
    for s in range(PLANE):
        column = marks[:CAP, s : s + 1]
        onehot[s * CAP : (s + 1) * CAP, :] = (column == lane).astype(F32).astype(BF16)
    centre = jnp.dot(onehot[...], cent[...], preferred_element_type=F32)
    held = jnp.sum((marks > 0.5).astype(F32), axis=0, keepdims=True)
    below = (
        lax.broadcasted_iota(jnp.int32, (PLANE, PLANE), 0)
        < lax.broadcasted_iota(jnp.int32, (PLANE, PLANE), 1)
    ).astype(F32)
    start = jnp.dot(held.astype(BF16), below.astype(BF16), preferred_element_type=F32)
    high = jnp.floor(start * (1.0 / CAP))
    low = start - high * CAP
    source = lax.shift_right_logical(lax.broadcasted_iota(jnp.int32, (PLANE, SLOTS), 1), 5)
    member = (lax.broadcasted_iota(jnp.int32, (PLANE, SLOTS), 0) == source).astype(F32).astype(BF16)

    def spread_out(row):
        return jnp.dot(row.astype(BF16), member, preferred_element_type=F32)

    within_source = (lax.broadcasted_iota(jnp.int32, (1, SLOTS), 1) & (CAP - 1)).astype(F32)
    place = jnp.where(
        within_source < spread_out(held),
        spread_out(high) * CAP + spread_out(low) + within_source,
        -1.0,
    )
    filled = jnp.sum(held, axis=1, keepdims=True)
    count[...] = jnp.broadcast_to(filled, (1, 128)).astype(jnp.int32)
    last = jnp.maximum(filled - 1.0, 0.0)
    for r in range(0, SLOTS, 256):
        row = (lax.broadcasted_iota(jnp.int32, (256, SLOTS), 0) + r).astype(F32)
        pick[r : r + 256, :] = (jnp.minimum(row, last) == place).astype(F32).astype(BF16)

    for e in (0, 1, 3, 2):
        land_second(e, 2)
    own[5].wait()
    await_bytes(recv.at[pl.ds(0, PLANE - 1)], ar)
    codes[...] = (recv[...].reshape(SLOTS, WIDTH).astype(F32) - centre).astype(BF16)
    results = [
        pltpu.make_async_copy(codes, codes_out, loc.at[6]),
        pltpu.make_async_copy(packed, packed_out, loc.at[7]),
        pltpu.make_async_copy(count, count_out, loc.at[8]),
    ]
    results[0].start()
    results[2].start()
    for r in range(0, SLOTS, 256):
        packed[r : r + 256, :] = jnp.dot(
            pick[r : r + 256, :], codes[...], preferred_element_type=F32
        ).astype(BF16)
    results[1].start()

    def shared(k):
        for half in range(2):
            await_bytes(half_rows(me, half), qc_r.at[half, k // 4, k % 4])

    each(0, 16, shared)

    await_bytes(wfull.at[pl.ds(0, 7 * 64)], ws.at[0])
    await_bytes(wfull.at[pl.ds(0, 7 * 64)], ws.at[1])
    await_bytes(q_out.at[pl.ds(0, 6 * PART)], qs.at[0])
    await_bytes(q_out.at[pl.ds(0, 24 * PART)], qs.at[1])
    await_bytes(q_out.at[pl.ds(0, 16 * ITEMS)], qs.at[2])
    await_bytes(slists.at[pl.ds(0, PLANE - 1)], ls)
    await_bytes(send.at[pl.ds(0, PLANE - 1)], av)
    for copy in results:
        copy.wait()


VARIANTS = (256, 512, 576, 640, 704, 768, 1024)
TILE = 4096


def score_kernel(count_ref, codes_ref, packed_ref, q_ref, out_ref, best_ref):
    count = count_ref[0, 0]

    @pl.when(pl.program_id(0) == 0)
    def _():
        out_ref[...] = codes_ref[...]

    for at, size in enumerate(VARIANTS):
        less = VARIANTS[at - 1] if at else 0

        @pl.when((count > less) & (count <= size))
        def _():
            for lo in range(0, TILE, 256):
                s = lax.dot_general(
                    packed_ref[:size, :], q_ref[lo : lo + 256, :], (((1,), (1,)), ((), ())),
                    preferred_element_type=F32,
                )
                best_ref[:, lo : lo + 256] = jnp.max(s, axis=0, keepdims=True)

    @pl.when(count == 0)
    def _():
        best_ref[...] = jnp.full_like(best_ref, -1e30)


def per_device(features, w_hidden, w_out, list_ids, centroids, queries):
    anywhere = pl.BlockSpec(memory_space=pl.ANY)
    dma = pltpu.SemaphoreType.DMA
    codes, packed, q_all, count = pl.pallas_call(
        kernel,
        out_shape=(
            jax.ShapeDtypeStruct((SLOTS, WIDTH), BF16),
            jax.ShapeDtypeStruct((SLOTS, WIDTH), BF16),
            jax.ShapeDtypeStruct((PLANE * ITEMS, WIDTH), BF16),
            jax.ShapeDtypeStruct((1, 128), jnp.int32),
        ),
        in_specs=[anywhere] * 6,
        out_specs=(anywhere,) * 4,
        scratch_shapes=[
            pltpu.VMEM((ITEMS, FEAT), BF16),
            pltpu.VMEM((FEAT, WCOLS), BF16),
            pltpu.VMEM((ITEMS, FEAT), BF16),
            pltpu.VMEM((ITEMS, FEAT), BF16),
            pltpu.VMEM((ITEMS, 128), F32),
            pltpu.VMEM((SLOTS, ITEMS), BF16),
            pltpu.VMEM((PLANE, CAP, WIDTH), BF16),
            pltpu.VMEM((PLANE, CAP, WIDTH), BF16),
            pltpu.VMEM((1, ITEMS), jnp.int32),
            pltpu.VMEM((LISTS, WIDTH), BF16),
            pltpu.VMEM((PLANE, 1, 128), F32),
            pltpu.VMEM((PLANE, 1, 128), F32),
            pltpu.VMEM((SLOTS, LISTS), BF16),
            pltpu.VMEM((SLOTS, WIDTH), BF16),
            pltpu.VMEM((SLOTS, SLOTS), BF16),
            pltpu.VMEM((SLOTS, WIDTH), BF16),
            pltpu.VMEM((1, 128), jnp.int32),
            dma((9,)), dma((2,)), dma((4, 3, 2)), dma((4, 3, 2)),
            dma((3,)), dma((2, 3)), dma((2, 4, 3)), dma((2, 4, 4)),
            dma, dma, dma, dma,
        ],
        compiler_params=pltpu.CompilerParams(
            collective_id=0, has_side_effects=True, vmem_limit_bytes=62 * 2**20
        ),
        name="encode_and_route",
    )(features, w_hidden, w_out, list_ids.reshape(1, ITEMS), centroids, queries)
    whole = pl.BlockSpec((SLOTS, WIDTH), lambda i: (0, 0))
    return pl.pallas_call(
        score_kernel,
        grid=(PLANE * ITEMS // TILE,),
        out_shape=(
            jax.ShapeDtypeStruct((SLOTS, WIDTH), BF16),
            jax.ShapeDtypeStruct((1, PLANE * ITEMS), F32),
        ),
        in_specs=[
            pl.BlockSpec(memory_space=pltpu.SMEM),
            whole,
            whole,
            pl.BlockSpec((TILE, WIDTH), lambda i: (i, 0)),
        ],
        out_specs=(whole, pl.BlockSpec((1, TILE), lambda i: (0, i))),
        compiler_params=pltpu.CompilerParams(vmem_limit_bytes=60 * 2**20),
        name="score",
    )(count, codes, packed, q_all)


def solution(mesh):
    in_specs = (
        P(("refresh", "lists"), None),
        P("refresh", None),
        P("refresh", None),
        P(("refresh", "lists")),
        P("lists", None),
        P("lists", None),
    )
    out_specs = (P(("refresh", "lists"), None), P(("refresh", "lists"), None))
    return jax.shard_map(
        per_device, mesh=mesh, in_specs=in_specs, out_specs=out_specs, check_vma=False
    )
```

```python
import jax
import jax.numpy as jnp
from jax import lax
from jax.experimental import pallas as pl
from jax.experimental.pallas import tpu as pltpu
from jax.sharding import PartitionSpec as P

MESH = pl.DeviceIdType.MESH
NY, NX, NC, NZ = 4, 4, 2, 8
PLANE = NY * NX * NC
ITEMS, FEAT, WIDTH, LISTS, CAP = 512, 1024, 256, 128, 32
SLOTS = PLANE * CAP
WCOLS = FEAT + WIDTH
STAGES = ((0, 512), (512, 512), (1024, 256))
ROWS = FEAT // NZ
PART = ITEMS // 2
F32, BF16 = jnp.float32, jnp.bfloat16


def kernel(
    feat_in, wh_in, wo_in, lists_in, cent_in, q_in,
    codes_out, packed_out, q_out, count_out,
    q_own, feat, wfull, normed, hid, squares, sel, send, recv, ids_ref, cent, slists, glists,
    codes, pick, packed, count,
    loc, ws, wz_r, wc_r, qs, q1_r, q2_r, qc_r, ls, lr, av, ar,
):
    me = lax.axis_index("lists")
    z = lax.axis_index("refresh")
    y, x, c = me // (NX * NC), (me // NC) % NX, me % NC

    def at(dy, dx, dc):
        return ((y + dy) % NY * NX + (x + dx) % NX) * NC + (c + dc) % NC

    def to(lists, refresh=None):
        return (z if refresh is None else refresh, lists)

    def push(src, dst, send_sem, recv_sem, device):
        pltpu.make_async_remote_copy(
            src_ref=src, dst_ref=dst, send_sem=send_sem, recv_sem=recv_sem,
            device_id=device, device_id_type=MESH,
        ).start()

    def await_bytes(ref, sem):
        pltpu.make_async_copy(ref, ref, sem).wait()

    def each(low, high, body):
        def step_once(i, _):
            body(i)
            return 0

        lax.fori_loop(low, high, step_once, 0)

    other = to(at(0, 0, 1))

    barrier = pltpu.get_barrier_semaphore()

    def peer_of(k):
        return at(k // 8, (k // 2) % 4, k % 2)

    def greet(device):
        pl.semaphore_signal(barrier, inc=1, device_id=device, device_id_type=MESH)

    each(1, PLANE, lambda k: greet(to(peer_of(k))))
    greet(to(me, (z + 1) % NZ))
    greet(to(me, (z + NZ - 1) % NZ))
    mine = pl.ds(pl.multiple_of(z * ROWS, ROWS), ROWS)
    q_mine = pl.ds(pl.multiple_of(me * ITEMS, ITEMS), ITEMS)
    own = [
        pltpu.make_async_copy(wh_in, wfull.at[mine, pl.ds(0, FEAT)], loc.at[0]),
        pltpu.make_async_copy(wo_in, wfull.at[mine, pl.ds(FEAT, WIDTH)], loc.at[1]),
        pltpu.make_async_copy(lists_in, ids_ref, loc.at[2]),
        pltpu.make_async_copy(feat_in, feat, loc.at[3]),
        pltpu.make_async_copy(cent_in, cent, loc.at[4]),
        pltpu.make_async_copy(q_in, q_own, loc.at[5]),
    ]
    for copy in own:
        copy.start()
    own[5].wait()
    keep_q = pltpu.make_async_copy(q_own, q_out.at[q_mine], loc.at[9])
    keep_q.start()
    pl.semaphore_wait(barrier, PLANE - 1 + 2)

    def shard(stage, plane, core, part=None):
        first, width = STAGES[stage]
        if part is not None:
            width //= 2
            first += part * width
        row = pl.multiple_of(plane * ROWS + core * (ROWS // 2), ROWS // 2)
        return wfull.at[pl.ds(row, ROWS // 2), pl.ds(first, width)]

    def source(hop, way):
        return (z + NZ - hop) % NZ if way == 0 else (z + hop) % NZ

    def pass_z(hop, stage, way):
        part = shard(stage, source(hop - 1, way), c, way if hop == 4 else None)
        there = to(me, (z + 1) % NZ if way == 0 else (z + NZ - 1) % NZ)
        src = part
        if hop == 1:
            first, width = STAGES[stage]
            held = wo_in if first == FEAT else wh_in
            src = held.at[
                pl.ds(pl.multiple_of(c * (ROWS // 2), ROWS // 2), ROWS // 2),
                pl.ds(first % FEAT, width),
            ]
        push(src, part, ws.at[0], wz_r.at[hop - 1, stage, way], there)

    def land_z(hop, stage):
        for way in range(2):
            part = shard(stage, source(hop, way), c, way if hop == 4 else None)
            await_bytes(part, wz_r.at[hop - 1, stage, way])
            if hop < 4:
                pass_z(hop + 1, stage, way)
        for way in range(2):
            part = shard(stage, source(hop, way), c, way if hop == 4 else None)
            push(part, part, ws.at[1], wc_r.at[hop - 1, stage, way], other)

    def paired(stage):
        for hop in range(1, 5):
            for way in range(2):
                part = shard(stage, source(hop, way), 1 - c, way if hop == 4 else None)
                await_bytes(part, wc_r.at[hop - 1, stage, way])

    def rows(block, first, size):
        return q_out.at[pl.ds(pl.multiple_of(block * ITEMS + first, 64), size)]

    def half_rows(block, half):
        return rows(block, half * PART, PART)

    def own_rows(half):
        return q_own.at[pl.ds(half * PART, PART)]

    def over(half, d):
        return to(at(d * half, d * (1 - half), 0))

    def block_of(half, e, d):
        return at(4 - d - half * (e - d), 4 - e - half * (d - e), 0)

    def first_leg(half, d):
        push(own_rows(half), half_rows(me, half), qs.at[0], q1_r.at[half, d - 1], over(half, d))

    def second_leg(half, e, d):
        here = half_rows(block_of(half, e, 0), half)
        src = here if e else own_rows(half)
        push(src, here, qs.at[1], q2_r.at[half, e, d - 1], over(1 - half, d))

    def share(half, e, d):
        here = half_rows(block_of(half, e, d), half)
        push(here, here, qs.at[2], qc_r.at[half, e, d], other)

    def land_first(e):
        for half in range(2):
            await_bytes(half_rows(me, half), q1_r.at[half, e - 1])
            share(half, e, 0)
            second_leg(half, e, 1)
            second_leg(half, e, 3)

    def land_second(e, d):
        for half in range(2):
            here = half_rows(block_of(half, e, d), half)
            await_bytes(here, q2_r.at[half, e, d - 1])
            if d == (1 if e < 2 else 3):
                push(here, here, qs.at[1], q2_r.at[half, e, 1], over(1 - half, d))
            share(half, e, d)

    for stage in range(3):
        pass_z(1, stage, 0)
        pass_z(1, stage, 1)
    for d in (1, 3, 2):
        for half in range(2):
            first_leg(half, d)
    for d in (1, 3):
        for half in range(2):
            second_leg(half, 0, d)
    for half in range(2):
        push(own_rows(half), half_rows(me, half), qs.at[2], qc_r.at[half, 0, 0], other)

    own[2].wait()
    ids = ids_ref[...]
    owner = lax.shift_right_logical(ids, 7)
    within = ids - owner * LISTS
    table = (lax.broadcasted_iota(jnp.int32, (PLANE, ITEMS), 0) == owner).astype(F32)
    earlier = (
        lax.broadcasted_iota(jnp.int32, (ITEMS, ITEMS), 0)
        < lax.broadcasted_iota(jnp.int32, (ITEMS, ITEMS), 1)
    ).astype(F32)
    prior = jnp.dot(table.astype(BF16), earlier.astype(BF16), preferred_element_type=F32)
    rank = jnp.sum(prior * table, axis=0, keepdims=True).astype(jnp.int32)
    rank_table = (lax.broadcasted_iota(jnp.int32, (128, ITEMS), 0) == rank).astype(F32)
    marked = table * (within + 1).astype(F32)
    slot_lists = lax.dot_general(
        marked.astype(BF16), rank_table.astype(BF16), (((1,), (1,)), ((), ())),
        preferred_element_type=F32,
    )
    slists[...] = slot_lists.reshape(PLANE, 1, 128)
    each(1, PLANE, lambda k: push(slists.at[peer_of(k)], glists.at[me], ls, lr, to(peer_of(k))))
    glists[me] = slists[me]

    for stage in range(3):
        land_z(1, stage)
    land_first(1)
    land_first(3)
    own[3].wait()

    def norm_rows(i):
        r = pl.ds(pl.multiple_of(i * 128, 128), 128)
        v = feat[r, :].astype(F32)
        scale = lax.rsqrt(jnp.mean(v * v, axis=-1, keepdims=True) + 1e-06)
        normed[r, :] = (v * scale).astype(BF16)

    each(0, ITEMS // 128, norm_rows)
    land_first(2)
    for stage in range(3):
        land_z(2, stage)
    land_second(0, 1)
    land_second(0, 3)
    slot = owner * CAP + rank

    def select(i):
        r = pl.multiple_of(i * 128, 128)
        row = lax.broadcasted_iota(jnp.int32, (128, ITEMS), 0) + r
        sel[pl.ds(r, 128), :] = (row == slot).astype(F32).astype(BF16)

    each(0, SLOTS // 128, select)
    for stage in range(3):
        land_z(3, stage)

    squares[...] = jnp.zeros_like(squares)

    def hidden(j):
        cols = pl.ds(pl.multiple_of(j * 256, 256), 256)
        pre = jnp.dot(normed[...], wfull[:, cols], preferred_element_type=F32)
        gelu = 0.5 * pre * (1.0 + lax.erf(pre * 0.7071067811865476))
        h = (feat[:, cols].astype(F32) + gelu).astype(BF16)
        hid[:, cols] = h
        h = h.astype(F32)
        h = h * h
        squares[...] += h[:, :128] + h[:, 128:]

    land_z(4, 0)
    own[0].wait()
    own[1].wait()
    paired(0)
    each(0, 2, hidden)
    land_z(4, 1)
    land_z(4, 2)
    paired(1)
    each(2, 4, hidden)
    paired(2)
    land_second(1, 1)
    land_second(3, 3)
    total = jnp.sum(squares[...], axis=-1, keepdims=True)
    scale = lax.rsqrt(total * (1.0 / FEAT) + 1e-06)
    out = jnp.dot(hid[...], wfull[:, FEAT:], preferred_element_type=F32)
    normed[:, :WIDTH] = (out * scale).astype(BF16)

    def route(i):
        dy = (i * 3 + 2) % 4
        there = (y + dy) % NY
        r = pl.multiple_of(there * 256, 256)
        out = jnp.dot(sel[pl.ds(r, 256), :], normed[:, :WIDTH], preferred_element_type=F32)
        send[pl.ds(there * 8, 8)] = out.astype(BF16).reshape(8, CAP, WIDTH)
        for dx in (2, 1, 3, 0):
            for dc in (1, 0):
                peer = at(dy, dx, dc)

                @pl.when(peer != me)
                def _():
                    push(send.at[peer], recv.at[me], av, ar, to(peer))

    each(0, 4, route)
    recv[me] = send[me]
    for e, d in ((2, 3), (1, 3), (3, 1), (2, 1)):
        land_second(e, d)

    own[4].wait()
    await_bytes(glists.at[pl.ds(0, PLANE - 1)], lr)
    marks = jnp.transpose(glists[...].reshape(PLANE, 128))
    held = jnp.sum((marks > 0.5).astype(F32), axis=0, keepdims=True)
    below = (
        lax.broadcasted_iota(jnp.int32, (PLANE, PLANE), 0)
        < lax.broadcasted_iota(jnp.int32, (PLANE, PLANE), 1)
    ).astype(F32)
    start = jnp.dot(held.astype(BF16), below.astype(BF16), preferred_element_type=F32)
    high = jnp.floor(start * (1.0 / CAP))
    low = start - high * CAP
    source = lax.shift_right_logical(lax.broadcasted_iota(jnp.int32, (PLANE, SLOTS), 1), 5)
    member = (lax.broadcasted_iota(jnp.int32, (PLANE, SLOTS), 0) == source).astype(F32).astype(BF16)

    def spread_out(row):
        return jnp.dot(row.astype(BF16), member, preferred_element_type=F32)

    within_source = (lax.broadcasted_iota(jnp.int32, (1, SLOTS), 1) & (CAP - 1)).astype(F32)
    place = jnp.where(
        within_source < spread_out(held),
        spread_out(high) * CAP + spread_out(low) + within_source,
        -1.0,
    )
    every = jnp.dot(marks[:CAP, :].astype(BF16), member, preferred_element_type=F32)
    ranks = lax.broadcasted_iota(jnp.int32, (CAP, SLOTS), 0).astype(F32)
    list_row = jnp.sum(jnp.where(ranks == within_source, every, 0.0), axis=0, keepdims=True)
    lists = lax.broadcasted_iota(jnp.int32, (LISTS, SLOTS), 0).astype(F32) + 1.0
    centre = lax.dot_general(
        (lists == list_row).astype(F32).astype(BF16), cent[...], (((0,), (0,)), ((), ())),
        preferred_element_type=F32,
    )
    filled = jnp.sum(held, axis=1, keepdims=True)
    count[...] = jnp.broadcast_to(filled, (1, 128)).astype(jnp.int32)
    last = jnp.maximum(filled - 1.0, 0.0)

    def choose(i):
        r = pl.multiple_of(i * 128, 128)
        row = (lax.broadcasted_iota(jnp.int32, (128, SLOTS), 0) + r).astype(F32)
        pick[pl.ds(r, 128), :] = (jnp.minimum(row, last) == place).astype(F32).astype(BF16)

    each(0, SLOTS // 128, choose)
    for e in (0, 1, 3, 2):
        land_second(e, 2)
    keep_q.wait()
    await_bytes(recv.at[pl.ds(0, PLANE - 1)], ar)
    codes[...] = (recv[...].reshape(SLOTS, WIDTH).astype(F32) - centre).astype(BF16)
    results = [
        pltpu.make_async_copy(codes, codes_out, loc.at[6]),
        pltpu.make_async_copy(packed, packed_out, loc.at[7]),
        pltpu.make_async_copy(count, count_out, loc.at[8]),
    ]
    results[0].start()
    results[2].start()

    def pack(i):
        r = pl.ds(pl.multiple_of(i * 256, 256), 256)
        packed[r, :] = jnp.dot(pick[r, :], codes[...], preferred_element_type=F32).astype(BF16)

    each(0, 4, pack)
    results[1].start()

    def shared(k):
        for half in range(2):
            await_bytes(half_rows(me, half), qc_r.at[half, k // 4, k % 4])

    each(0, 16, shared)

    await_bytes(wfull.at[pl.ds(0, 7 * 64)], ws.at[0])
    await_bytes(wfull.at[pl.ds(0, 7 * 64)], ws.at[1])
    await_bytes(q_out.at[pl.ds(0, 6 * PART)], qs.at[0])
    await_bytes(q_out.at[pl.ds(0, 24 * PART)], qs.at[1])
    await_bytes(q_out.at[pl.ds(0, 16 * ITEMS)], qs.at[2])
    await_bytes(slists.at[pl.ds(0, PLANE - 1)], ls)
    await_bytes(send.at[pl.ds(0, PLANE - 1)], av)
    for copy in results:
        copy.wait()


VARIANTS = (256, 512, 544, 576, 608, 640, 704, 768, 1024)
TILE = 4096


def score_kernel(count_ref, codes_ref, packed_ref, q_ref, out_ref, best_ref):
    count = count_ref[0, 0]

    out_ref[...] = codes_ref[...]

    for at, size in enumerate(VARIANTS):
        less = VARIANTS[at - 1] if at else 0

        @pl.when((count > less) & (count <= size))
        def _():
            for lo in range(0, TILE, 256):
                s = lax.dot_general(
                    packed_ref[:size, :], q_ref[lo : lo + 256, :], (((1,), (1,)), ((), ())),
                    preferred_element_type=F32,
                )
                best_ref[:, lo : lo + 256] = jnp.max(s, axis=0, keepdims=True)

    @pl.when(count == 0)
    def _():
        best_ref[...] = jnp.full_like(best_ref, -1e30)


def per_device(features, w_hidden, w_out, list_ids, centroids, queries):
    anywhere = pl.BlockSpec(memory_space=pl.ANY)
    dma = pltpu.SemaphoreType.DMA
    codes, packed, q_all, count = pl.pallas_call(
        kernel,
        out_shape=(
            jax.ShapeDtypeStruct((SLOTS, WIDTH), BF16),
            jax.ShapeDtypeStruct((SLOTS, WIDTH), BF16),
            jax.ShapeDtypeStruct((PLANE * ITEMS, WIDTH), BF16),
            jax.ShapeDtypeStruct((1, 128), jnp.int32),
        ),
        in_specs=[anywhere] * 6,
        out_specs=(anywhere,) * 4,
        scratch_shapes=[
            pltpu.VMEM((ITEMS, WIDTH), BF16),
            pltpu.VMEM((ITEMS, FEAT), BF16),
            pltpu.VMEM((FEAT, WCOLS), BF16),
            pltpu.VMEM((ITEMS, FEAT), BF16),
            pltpu.VMEM((ITEMS, FEAT), BF16),
            pltpu.VMEM((ITEMS, 128), F32),
            pltpu.VMEM((SLOTS, ITEMS), BF16),
            pltpu.VMEM((PLANE, CAP, WIDTH), BF16),
            pltpu.VMEM((PLANE, CAP, WIDTH), BF16),
            pltpu.VMEM((1, ITEMS), jnp.int32),
            pltpu.VMEM((LISTS, WIDTH), BF16),
            pltpu.VMEM((PLANE, 1, 128), F32),
            pltpu.VMEM((PLANE, 1, 128), F32),
            pltpu.VMEM((SLOTS, WIDTH), BF16),
            pltpu.VMEM((SLOTS, SLOTS), BF16),
            pltpu.VMEM((SLOTS, WIDTH), BF16),
            pltpu.VMEM((1, 128), jnp.int32),
            dma((10,)), dma((2,)), dma((4, 3, 2)), dma((4, 3, 2)),
            dma((3,)), dma((2, 3)), dma((2, 4, 3)), dma((2, 4, 4)),
            dma, dma, dma, dma,
        ],
        compiler_params=pltpu.CompilerParams(
            collective_id=0, has_side_effects=True, vmem_limit_bytes=62 * 2**20
        ),
        name="encode_and_route",
    )(features, w_hidden, w_out, list_ids.reshape(1, ITEMS), centroids, queries)
    steps = PLANE * ITEMS // TILE
    part = pl.BlockSpec((SLOTS // steps, WIDTH), lambda i: (i, 0))
    return pl.pallas_call(
        score_kernel,
        grid=(steps,),
        out_shape=(
            jax.ShapeDtypeStruct((SLOTS, WIDTH), BF16),
            jax.ShapeDtypeStruct((1, PLANE * ITEMS), F32),
        ),
        in_specs=[
            pl.BlockSpec(memory_space=pltpu.SMEM),
            part,
            pl.BlockSpec((SLOTS, WIDTH), lambda i: (0, 0)),
            pl.BlockSpec((TILE, WIDTH), lambda i: (i, 0)),
        ],
        out_specs=(part, pl.BlockSpec((1, TILE), lambda i: (0, i))),
        compiler_params=pltpu.CompilerParams(vmem_limit_bytes=60 * 2**20),
        name="score",
    )(count, codes, packed, q_all)


def solution(mesh):
    in_specs = (
        P(("refresh", "lists"), None),
        P("refresh", None),
        P("refresh", None),
        P(("refresh", "lists")),
        P("lists", None),
        P("lists", None),
    )
    out_specs = (P(("refresh", "lists"), None), P(("refresh", "lists"), None))
    return jax.shard_map(
        per_device, mesh=mesh, in_specs=in_specs, out_specs=out_specs, check_vma=False
    )
```

```python
import jax
import jax.numpy as jnp
from jax import lax
from jax.experimental import pallas as pl
from jax.experimental.pallas import tpu as pltpu
from jax.sharding import PartitionSpec as P

MESH = pl.DeviceIdType.MESH
NY, NX, NC, NZ = 4, 4, 2, 8
PLANE = NY * NX * NC
ITEMS, FEAT, WIDTH, LISTS, CAP = 512, 1024, 256, 128, 32
SLOTS = PLANE * CAP
WCOLS = FEAT + WIDTH
STAGES = ((0, 512), (512, 512), (1024, 256))
ROWS = FEAT // NZ
PART = ITEMS // 2
F32, BF16 = jnp.float32, jnp.bfloat16


def kernel(
    feat_in, wh_in, wo_in, lists_in, cent_in, q_in,
    codes_out, packed_out, q_out, count_out,
    q_own, feat, wfull, normed, hid, squares, sel, send, recv, ids_ref, cent, slists, glists,
    codes, pick, packed, count,
    loc, ws, wz_r, wc_r, qs, q1_r, q2_r, qc_r, ls, lr, av, ar,
):
    me = lax.axis_index("lists")
    z = lax.axis_index("refresh")
    y, x, c = me // (NX * NC), (me // NC) % NX, me % NC

    def at(dy, dx, dc):
        return ((y + dy) % NY * NX + (x + dx) % NX) * NC + (c + dc) % NC

    def to(lists, refresh=None):
        return (z if refresh is None else refresh, lists)

    def push(src, dst, send_sem, recv_sem, device):
        pltpu.make_async_remote_copy(
            src_ref=src, dst_ref=dst, send_sem=send_sem, recv_sem=recv_sem,
            device_id=device, device_id_type=MESH,
        ).start()

    def await_bytes(ref, sem):
        pltpu.make_async_copy(ref, ref, sem).wait()

    def each(low, high, body):
        def step_once(i, _):
            body(i)
            return 0

        lax.fori_loop(low, high, step_once, 0)

    other = to(at(0, 0, 1))

    barrier = pltpu.get_barrier_semaphore()

    def peer_of(k):
        return at(k // 8, (k // 2) % 4, k % 2)

    def greet(device):
        pl.semaphore_signal(barrier, inc=1, device_id=device, device_id_type=MESH)

    each(1, PLANE, lambda k: greet(to(peer_of(k))))
    greet(to(me, (z + 1) % NZ))
    greet(to(me, (z + NZ - 1) % NZ))
    mine = pl.ds(pl.multiple_of(z * ROWS, ROWS), ROWS)
    q_mine = pl.ds(pl.multiple_of(me * ITEMS, ITEMS), ITEMS)
    own = [
        pltpu.make_async_copy(wh_in, wfull.at[mine, pl.ds(0, FEAT)], loc.at[0]),
        pltpu.make_async_copy(wo_in, wfull.at[mine, pl.ds(FEAT, WIDTH)], loc.at[1]),
        pltpu.make_async_copy(lists_in, ids_ref, loc.at[2]),
        pltpu.make_async_copy(feat_in, feat, loc.at[3]),
        pltpu.make_async_copy(cent_in, cent, loc.at[4]),
        pltpu.make_async_copy(q_in, q_own, loc.at[5]),
    ]
    for copy in own:
        copy.start()
    own[5].wait()
    keep_q = pltpu.make_async_copy(q_own, q_out.at[q_mine], loc.at[9])
    keep_q.start()
    pl.semaphore_wait(barrier, PLANE - 1 + 2)

    def shard(stage, plane, core, part=None):
        first, width = STAGES[stage]
        if part is not None:
            width //= 2
            first += part * width
        row = pl.multiple_of(plane * ROWS + core * (ROWS // 2), ROWS // 2)
        return wfull.at[pl.ds(row, ROWS // 2), pl.ds(first, width)]

    def source(hop, way):
        return (z + NZ - hop) % NZ if way == 0 else (z + hop) % NZ

    def pass_z(hop, stage, way):
        part = shard(stage, source(hop - 1, way), c, way if hop == 4 else None)
        there = to(me, (z + 1) % NZ if way == 0 else (z + NZ - 1) % NZ)
        src = part
        if hop == 1:
            first, width = STAGES[stage]
            held = wo_in if first == FEAT else wh_in
            src = held.at[
                pl.ds(pl.multiple_of(c * (ROWS // 2), ROWS // 2), ROWS // 2),
                pl.ds(first % FEAT, width),
            ]
        push(src, part, ws.at[0], wz_r.at[hop - 1, stage, way], there)

    def land_z(hop, stage):
        for way in range(2):
            part = shard(stage, source(hop, way), c, way if hop == 4 else None)
            await_bytes(part, wz_r.at[hop - 1, stage, way])
            if hop < 4:
                pass_z(hop + 1, stage, way)
        for way in range(2):
            part = shard(stage, source(hop, way), c, way if hop == 4 else None)
            push(part, part, ws.at[1], wc_r.at[hop - 1, stage, way], other)

    def paired(stage):
        for hop in range(1, 5):
            for way in range(2):
                part = shard(stage, source(hop, way), 1 - c, way if hop == 4 else None)
                await_bytes(part, wc_r.at[hop - 1, stage, way])

    def rows(block, first, size):
        return q_out.at[pl.ds(pl.multiple_of(block * ITEMS + first, 64), size)]

    def half_rows(block, half):
        return rows(block, half * PART, PART)

    def own_rows(half):
        return q_own.at[pl.ds(half * PART, PART)]

    def over(half, d):
        return to(at(d * half, d * (1 - half), 0))

    def block_of(half, e, d):
        return at(4 - d - half * (e - d), 4 - e - half * (d - e), 0)

    def first_leg(half, d):
        push(own_rows(half), half_rows(me, half), qs.at[0], q1_r.at[half, d - 1], over(half, d))

    def second_leg(half, e, d):
        here = half_rows(block_of(half, e, 0), half)
        src = here if e else own_rows(half)
        push(src, here, qs.at[1], q2_r.at[half, e, d - 1], over(1 - half, d))

    def share(half, e, d):
        here = half_rows(block_of(half, e, d), half)
        push(here, here, qs.at[2], qc_r.at[half, e, d], other)

    def land_first(e):
        for half in range(2):
            await_bytes(half_rows(me, half), q1_r.at[half, e - 1])
            share(half, e, 0)
            second_leg(half, e, 1)
            second_leg(half, e, 3)

    def land_second(e, d):
        for half in range(2):
            here = half_rows(block_of(half, e, d), half)
            await_bytes(here, q2_r.at[half, e, d - 1])
            if d == (1 if e < 2 else 3):
                push(here, here, qs.at[1], q2_r.at[half, e, 1], over(1 - half, d))
            share(half, e, d)

    for stage in range(3):
        pass_z(1, stage, 0)
        pass_z(1, stage, 1)
    for d in (1, 3, 2):
        for half in range(2):
            first_leg(half, d)
    for d in (1, 3):
        for half in range(2):
            second_leg(half, 0, d)
    for half in range(2):
        push(own_rows(half), half_rows(me, half), qs.at[2], qc_r.at[half, 0, 0], other)

    own[2].wait()
    ids = ids_ref[...]
    owner = lax.shift_right_logical(ids, 7)
    within = ids - owner * LISTS
    table = (lax.broadcasted_iota(jnp.int32, (PLANE, ITEMS), 0) == owner).astype(F32)
    earlier = (
        lax.broadcasted_iota(jnp.int32, (ITEMS, ITEMS), 0)
        < lax.broadcasted_iota(jnp.int32, (ITEMS, ITEMS), 1)
    ).astype(F32)
    prior = jnp.dot(table.astype(BF16), earlier.astype(BF16), preferred_element_type=F32)
    rank = jnp.sum(prior * table, axis=0, keepdims=True).astype(jnp.int32)
    rank_table = (lax.broadcasted_iota(jnp.int32, (128, ITEMS), 0) == rank).astype(F32)
    marked = table * (within + 1).astype(F32)
    slot_lists = lax.dot_general(
        marked.astype(BF16), rank_table.astype(BF16), (((1,), (1,)), ((), ())),
        preferred_element_type=F32,
    )
    slists[...] = slot_lists.reshape(PLANE, 1, 128)
    each(1, PLANE, lambda k: push(slists.at[peer_of(k)], glists.at[me], ls, lr, to(peer_of(k))))
    glists[me] = slists[me]

    for stage in range(3):
        land_z(1, stage)
    land_first(1)
    land_first(3)
    own[3].wait()

    def norm_rows(i):
        r = pl.ds(pl.multiple_of(i * 128, 128), 128)
        v = feat[r, :].astype(F32)
        scale = lax.rsqrt(jnp.mean(v * v, axis=-1, keepdims=True) + 1e-06)
        normed[r, :] = (v * scale).astype(BF16)

    each(0, ITEMS // 128, norm_rows)
    land_first(2)
    for stage in range(3):
        land_z(2, stage)
    land_second(0, 1)
    land_second(0, 3)
    slot = owner * CAP + rank

    def select(i):
        r = pl.multiple_of(i * 128, 128)
        row = lax.broadcasted_iota(jnp.int32, (128, ITEMS), 0) + r
        sel[pl.ds(r, 128), :] = (row == slot).astype(F32).astype(BF16)

    each(0, SLOTS // 128, select)
    for stage in range(3):
        land_z(3, stage)

    squares[...] = jnp.zeros_like(squares)

    def hidden(j):
        cols = pl.ds(pl.multiple_of(j * 256, 256), 256)
        pre = jnp.dot(normed[...], wfull[:, cols], preferred_element_type=F32)
        gelu = 0.5 * pre * (1.0 + lax.erf(pre * 0.7071067811865476))
        h = (feat[:, cols].astype(F32) + gelu).astype(BF16)
        hid[:, cols] = h
        h = h.astype(F32)
        h = h * h
        squares[...] += h[:, :128] + h[:, 128:]

    land_z(4, 0)
    own[0].wait()
    own[1].wait()
    paired(0)
    each(0, 2, hidden)
    land_z(4, 1)
    land_z(4, 2)
    paired(1)
    each(2, 4, hidden)
    paired(2)
    land_second(1, 1)
    land_second(3, 3)
    total = jnp.sum(squares[...], axis=-1, keepdims=True)
    scale = lax.rsqrt(total * (1.0 / FEAT) + 1e-06)
    out = jnp.dot(hid[...], wfull[:, FEAT:], preferred_element_type=F32)
    normed[:, :WIDTH] = (out * scale).astype(BF16)

    def route(i):
        dy = (i * 3 + 2) % 4
        there = (y + dy) % NY
        r = pl.multiple_of(there * 256, 256)
        out = jnp.dot(sel[pl.ds(r, 256), :], normed[:, :WIDTH], preferred_element_type=F32)
        send[pl.ds(there * 8, 8)] = out.astype(BF16).reshape(8, CAP, WIDTH)
        for dx in (2, 1, 3, 0):
            for dc in (1, 0):
                peer = at(dy, dx, dc)

                @pl.when(peer != me)
                def _():
                    push(send.at[peer], recv.at[me], av, ar, to(peer))

    each(0, 4, route)
    recv[me] = send[me]
    for e, d in ((2, 3), (1, 3), (3, 1), (2, 1)):
        land_second(e, d)

    own[4].wait()
    await_bytes(glists.at[pl.ds(0, PLANE - 1)], lr)
    marks = jnp.transpose(glists[...].reshape(PLANE, 128))
    held = jnp.sum((marks > 0.5).astype(F32), axis=0, keepdims=True)
    below = (
        lax.broadcasted_iota(jnp.int32, (PLANE, PLANE), 0)
        < lax.broadcasted_iota(jnp.int32, (PLANE, PLANE), 1)
    ).astype(F32)
    start = jnp.dot(held.astype(BF16), below.astype(BF16), preferred_element_type=F32)
    high = jnp.floor(start * (1.0 / CAP))
    low = start - high * CAP
    source = lax.shift_right_logical(lax.broadcasted_iota(jnp.int32, (PLANE, SLOTS), 1), 5)
    member = (lax.broadcasted_iota(jnp.int32, (PLANE, SLOTS), 0) == source).astype(F32).astype(BF16)

    def spread_out(row):
        return jnp.dot(row.astype(BF16), member, preferred_element_type=F32)

    within_source = (lax.broadcasted_iota(jnp.int32, (1, SLOTS), 1) & (CAP - 1)).astype(F32)
    place = jnp.where(
        within_source < spread_out(held),
        spread_out(high) * CAP + spread_out(low) + within_source,
        -1.0,
    )
    every = jnp.dot(marks[:CAP, :].astype(BF16), member, preferred_element_type=F32)
    ranks = lax.broadcasted_iota(jnp.int32, (CAP, SLOTS), 0).astype(F32)
    list_row = jnp.sum(jnp.where(ranks == within_source, every, 0.0), axis=0, keepdims=True)
    lists = lax.broadcasted_iota(jnp.int32, (LISTS, SLOTS), 0).astype(F32) + 1.0
    centre = lax.dot_general(
        (lists == list_row).astype(F32).astype(BF16), cent[...], (((0,), (0,)), ((), ())),
        preferred_element_type=F32,
    )
    filled = jnp.sum(held, axis=1, keepdims=True)
    count[...] = jnp.broadcast_to(filled, (1, 128)).astype(jnp.int32)
    last = jnp.maximum(filled - 1.0, 0.0)

    def choose(i):
        r = pl.multiple_of(i * 128, 128)
        row = (lax.broadcasted_iota(jnp.int32, (128, SLOTS), 0) + r).astype(F32)
        pick[pl.ds(r, 128), :] = (jnp.minimum(row, last) == place).astype(F32).astype(BF16)

    each(0, SLOTS // 128, choose)
    for e in (0, 1, 3, 2):
        land_second(e, 2)
    keep_q.wait()
    await_bytes(recv.at[pl.ds(0, PLANE - 1)], ar)
    codes[...] = (recv[...].reshape(SLOTS, WIDTH).astype(F32) - centre).astype(BF16)
    results = [
        pltpu.make_async_copy(codes, codes_out, loc.at[6]),
        pltpu.make_async_copy(packed, packed_out, loc.at[7]),
        pltpu.make_async_copy(count, count_out, loc.at[8]),
    ]
    results[0].start()
    results[2].start()

    def pack(i):
        r = pl.ds(pl.multiple_of(i * 256, 256), 256)
        packed[r, :] = jnp.dot(pick[r, :], codes[...], preferred_element_type=F32).astype(BF16)
        pltpu.make_async_copy(packed.at[r], packed_out.at[r], loc.at[7]).start()

    each(0, 4, pack)

    def shared(k):
        for half in range(2):
            await_bytes(half_rows(me, half), qc_r.at[half, k // 4, k % 4])

    each(0, 16, shared)

    await_bytes(wfull.at[pl.ds(0, 7 * 64)], ws.at[0])
    await_bytes(wfull.at[pl.ds(0, 7 * 64)], ws.at[1])
    await_bytes(q_out.at[pl.ds(0, 6 * PART)], qs.at[0])
    await_bytes(q_out.at[pl.ds(0, 24 * PART)], qs.at[1])
    await_bytes(q_out.at[pl.ds(0, 16 * ITEMS)], qs.at[2])
    await_bytes(slists.at[pl.ds(0, PLANE - 1)], ls)
    await_bytes(send.at[pl.ds(0, PLANE - 1)], av)
    for copy in results:
        copy.wait()


VARIANTS = (256, 512, 544, 576, 608, 640, 704, 768, 1024)
TILE = 4096


def score_kernel(count_ref, codes_ref, packed_ref, q_ref, out_ref, best_ref):
    count = count_ref[0, 0]

    out_ref[...] = codes_ref[...]

    for at, size in enumerate(VARIANTS):
        less = VARIANTS[at - 1] if at else 0

        @pl.when((count > less) & (count <= size))
        def _():
            for lo in range(0, TILE, 256):
                s = lax.dot_general(
                    packed_ref[:size, :], q_ref[lo : lo + 256, :], (((1,), (1,)), ((), ())),
                    preferred_element_type=F32,
                )
                best_ref[:, lo : lo + 256] = jnp.max(s, axis=0, keepdims=True)

    @pl.when(count == 0)
    def _():
        best_ref[...] = jnp.full_like(best_ref, -1e30)


def per_device(features, w_hidden, w_out, list_ids, centroids, queries):
    anywhere = pl.BlockSpec(memory_space=pl.ANY)
    dma = pltpu.SemaphoreType.DMA
    codes, packed, q_all, count = pl.pallas_call(
        kernel,
        out_shape=(
            jax.ShapeDtypeStruct((SLOTS, WIDTH), BF16),
            jax.ShapeDtypeStruct((SLOTS, WIDTH), BF16),
            jax.ShapeDtypeStruct((PLANE * ITEMS, WIDTH), BF16),
            jax.ShapeDtypeStruct((1, 128), jnp.int32),
        ),
        in_specs=[anywhere] * 6,
        out_specs=(anywhere,) * 4,
        scratch_shapes=[
            pltpu.VMEM((ITEMS, WIDTH), BF16),
            pltpu.VMEM((ITEMS, FEAT), BF16),
            pltpu.VMEM((FEAT, WCOLS), BF16),
            pltpu.VMEM((ITEMS, FEAT), BF16),
            pltpu.VMEM((ITEMS, FEAT), BF16),
            pltpu.VMEM((ITEMS, 128), F32),
            pltpu.VMEM((SLOTS, ITEMS), BF16),
            pltpu.VMEM((PLANE, CAP, WIDTH), BF16),
            pltpu.VMEM((PLANE, CAP, WIDTH), BF16),
            pltpu.VMEM((1, ITEMS), jnp.int32),
            pltpu.VMEM((LISTS, WIDTH), BF16),
            pltpu.VMEM((PLANE, 1, 128), F32),
            pltpu.VMEM((PLANE, 1, 128), F32),
            pltpu.VMEM((SLOTS, WIDTH), BF16),
            pltpu.VMEM((SLOTS, SLOTS), BF16),
            pltpu.VMEM((SLOTS, WIDTH), BF16),
            pltpu.VMEM((1, 128), jnp.int32),
            dma((10,)), dma((2,)), dma((4, 3, 2)), dma((4, 3, 2)),
            dma((3,)), dma((2, 3)), dma((2, 4, 3)), dma((2, 4, 4)),
            dma, dma, dma, dma,
        ],
        compiler_params=pltpu.CompilerParams(
            collective_id=0, has_side_effects=True, vmem_limit_bytes=62 * 2**20
        ),
        name="encode_and_route",
    )(features, w_hidden, w_out, list_ids.reshape(1, ITEMS), centroids, queries)
    steps = PLANE * ITEMS // TILE
    part = pl.BlockSpec((SLOTS // steps, WIDTH), lambda i: (i, 0))
    return pl.pallas_call(
        score_kernel,
        grid=(steps,),
        out_shape=(
            jax.ShapeDtypeStruct((SLOTS, WIDTH), BF16),
            jax.ShapeDtypeStruct((1, PLANE * ITEMS), F32),
        ),
        in_specs=[
            pl.BlockSpec(memory_space=pltpu.SMEM),
            part,
            pl.BlockSpec((SLOTS, WIDTH), lambda i: (0, 0)),
            pl.BlockSpec((TILE, WIDTH), lambda i: (i, 0)),
        ],
        out_specs=(part, pl.BlockSpec((1, TILE), lambda i: (0, i))),
        compiler_params=pltpu.CompilerParams(vmem_limit_bytes=60 * 2**20),
        name="score",
    )(count, codes, packed, q_all)


def solution(mesh):
    in_specs = (
        P(("refresh", "lists"), None),
        P("refresh", None),
        P("refresh", None),
        P(("refresh", "lists")),
        P("lists", None),
        P("lists", None),
    )
    out_specs = (P(("refresh", "lists"), None), P(("refresh", "lists"), None))
    return jax.shard_map(
        per_device, mesh=mesh, in_specs=in_specs, out_specs=out_specs, check_vma=False
    )
```
